256 devices in a mesh: gx: 8 (over z_lo, core), gy: 32 (over z_hi, x, y).
Axes of the slice: x: 4, y: 4, z: 8 (z_hi: 2, z_lo: 4; z = z_hi * 4 + z_lo), core: 2. Of those that a mesh axis runs over, the one named last changes fastest.
Arguments:
- positions: float32 [3, 131072], P(None, ('gx', 'gy')), may hold values from 0 to 1
- species: int32 [131072], P(('gx', 'gy')), may hold values from 0 to 7, as said below
- neighbours: int32 [131072, 32], P(('gx', 'gy')), may hold values from -1 to 2815, as said below
- ghost_index: int32 [65536], P(('gx', 'gy')), may hold values from 0 to 511, as said below
- wave_index: int32 [3, 4096], replicated, may hold values from -32 to 31, as said below
- embedding: float32 [8, 128], replicated, may hold values from -6 to 6
- radial_weight: float32 [8, 256], replicated, may hold values from -2 to 2
- message_weight: float32 [128, 128], replicated, may hold values from -0.5 to 0.5
- scalar_weight: float32 [128, 128], replicated, may hold values from -0.5 to 0.5
- vector_weight: float32 [128, 128], replicated, may hold values from -0.25 to 0.25
- readout_hidden: float32 [128, 128], replicated, may hold values from -0.5 to 0.5
- readout_vector: float32 [128], replicated, may hold values from -0.5 to 0.5
- charge_weight: float32 [128, 32], replicated, may hold values from -0.5 to 0.5
Outputs:
- forces: float32 [3, 131072], P(None, ('gx', 'gy'))
- atom_energy: float32 [131072], P(('gx', 'gy'))
The draws below stay inside these ranges and needn't reach their ends.
Inputs may be any that keep to these rules, and one draw needn't show every extreme that they name: Each atom's species. Within each domain, atoms are more often of the lower half of the species the higher the domain number d is. `ghost_index`: within each domain's block, 256 different local atom indices. `neighbours`: entries below 512 are the domain's own atoms, never the atom itself; an entry 512 + 256 b + g is entry g of the b-th received boundary block, b = 3 i + j, never b = 4; -1 pads the slots after the live ones; each row has 16 to 32 live slots, the first atom of every domain 32. `wave_index`: the 4096 columns are distinct integer vectors; row 0 lies in -8 to 8, row 1 in -32 to 31, row 2 in 1 to 4.
All inputs are finite; a program needn't handle non-finite values.
Results may differ from the reference program's by a relative error of at most 0.0003.
Values sent between devices are 32-bit elements; how exact they have to be, the bound alone decides.
No kernel may reach another device: no remote copies, remote signals or barrier semaphores. Data moves between devices by JAX's collectives and lax.ppermute only.
A program may use at most 128 MiB of HBM per device.

```python
import jax
import jax.numpy as jnp
from jax import lax

C = 128
NB = 8
Q = 32
KV = 4096
NS = 8
K = 32
A_DEV = 512
G = 256
ATOMS = 131072
GHOSTS = 65536
N_GX = 8
N_GY = 32


def draw_species(key, part):
    key = jax.random.fold_in(key, 11)
    first_key, second_key, third_key = jax.random.split(key, 3)
    domain = jnp.arange(ATOMS, dtype=jnp.int32) // A_DEV
    domains = ATOMS // A_DEV
    cutoff = 100 + 800 * domain // max(domains - 1, 1)
    chance = jax.random.randint(first_key, (ATOMS,), 0, 1000)
    light_kind = jax.random.randint(second_key, (ATOMS,), 0, NS // 2)
    heavy_kind = jax.random.randint(third_key, (ATOMS,), NS // 2, NS)
    return jnp.where(chance < cutoff, light_kind, heavy_kind).astype(jnp.int32)


def draw_ghost_index(key, part):
    key = jax.random.fold_in(key, 12)
    domains = GHOSTS // G
    keys_all = jax.random.split(key, domains)
    picked = jax.vmap(lambda sub_key: jax.random.permutation(sub_key, A_DEV)[:G])(keys_all)
    return picked.reshape(GHOSTS).astype(jnp.int32)


def draw_neighbours(key, part):
    key = jax.random.fold_in(key, 13)
    count_key, pick_key = jax.random.split(key)
    local_index = jnp.arange(ATOMS, dtype=jnp.int32) % A_DEV
    counts = jax.random.randint(count_key, (ATOMS,), K // 2, K + 1)
    counts = jnp.where(local_index == 0, K, counts)
    picks = jax.random.randint(pick_key, (ATOMS, K), 0, A_DEV + 8 * G)
    own_pick = jnp.where(picks == local_index[:, None], (picks + 1) % A_DEV, picks)
    border_pick = picks - A_DEV
    block_number = border_pick // G
    block_number = block_number + (block_number >= 4).astype(jnp.int32)
    far_pick = A_DEV + block_number * G + border_pick % G
    chosen = jnp.where(picks < A_DEV, own_pick, far_pick)
    slots = jnp.arange(K, dtype=jnp.int32)
    return jnp.where(slots[None, :] < counts[:, None], chosen, -1).astype(jnp.int32)


def draw_wave_index(key, part):
    key = jax.random.fold_in(key, 14)
    point_count = 17 * 64 * 4
    lattice_index = jnp.arange(point_count, dtype=jnp.int32)
    along_first = lattice_index // 256 - 8
    along_second = lattice_index // 4 % 64 - 32
    along_third = lattice_index % 4 + 1
    metric = 16 * along_first * along_first + along_second * along_second + 64 * along_third * along_third
    tie_break = jax.random.permutation(key, point_count).astype(jnp.int32)
    scores = metric * 8192 + tie_break
    scores = jnp.where(lattice_index == 0, -2, jnp.where(lattice_index == point_count - 1, -1, scores))
    picked = jnp.argsort(scores, stable=True)[:KV]
    return jnp.stack([along_first[picked], along_second[picked], along_third[picked]]).astype(jnp.int32)


def block_levels(own_key, shape, shards, least, high):
    loudness, own = 1.0, jax.random.fold_in(own_key, 6)
    for position, parts in shards:
        draws = jnp.exp(jax.random.uniform(jax.random.fold_in(own, position), (parts,), jnp.float32, least / len(shards), high / len(shards)))
        loudness = loudness * jnp.repeat(draws, shape[position] // parts).reshape([-1 if axis == position else 1 for axis in range(len(shape))])
    return loudness


def bell_draw(own_key, dims, spread, bound, kind=jnp.bfloat16):
    return jnp.clip(spread * jax.random.normal(own_key, dims, jnp.float32), -bound, bound).astype(kind)


def setup_inputs(seed: int = 0) -> dict:
    key_list = jax.random.split(jax.random.key(seed), 14)
    positions = jnp.clip(1.0 * jax.random.uniform(key_list[0], (3, ATOMS), jnp.float32) ** block_levels(key_list[0], (3, ATOMS), ((1, 256),), -0.2, 0.2), 0.0, 1.0)
    species = draw_species(jax.random.fold_in(key_list[13], 71), 0)
    neighbours = draw_neighbours(jax.random.fold_in(key_list[13], 71), 0)
    ghost_index = draw_ghost_index(jax.random.fold_in(key_list[13], 71), 0)
    wave_index = draw_wave_index(jax.random.fold_in(key_list[13], 71), 0)
    embedding = bell_draw(key_list[5], (NS, C), 1.0, 6.0, jnp.float32)
    radial_weight = bell_draw(key_list[6], (NB, 2 * C), NB ** -0.5, 2.0, jnp.float32)
    message_weight = bell_draw(key_list[7], (C, C), C ** -0.5, 0.5, jnp.float32)
    scalar_weight = bell_draw(key_list[8], (C, C), C ** -0.5, 0.5, jnp.float32)
    vector_weight = bell_draw(key_list[9], (C, C), (4 * C) ** -0.5, 0.25, jnp.float32)
    readout_hidden = bell_draw(key_list[10], (C, C), C ** -0.5, 0.5, jnp.float32)
    readout_vector = bell_draw(key_list[11], (C,), C ** -0.5, 0.5, jnp.float32)
    charge_weight = bell_draw(key_list[12], (C, Q), C ** -0.5, 0.5, jnp.float32)
    return dict(positions=positions, species=species, neighbours=neighbours, ghost_index=ghost_index, wave_index=wave_index, embedding=embedding, radial_weight=radial_weight, message_weight=message_weight, scalar_weight=scalar_weight, vector_weight=vector_weight, readout_hidden=readout_hidden, readout_vector=readout_vector, charge_weight=charge_weight)


HIGHEST = lax.Precision.HIGHEST
TWO_PI = 6.283185307179586
BOX_HEIGHT = 4.0
SPLITTING = 2.5
SOFTENING = 0.01
CENTRE_STEP = 0.3

def short_range(own_pos, table_pos, one_hot, neighbours, embedding, radial_weight, message_weight, scalar_weight, vector_weight, readout_hidden, readout_vector, charge_weight):
    atom_count = own_pos.shape[1]
    channels = embedding.shape[1]
    feature_table = jnp.dot(one_hot, embedding, precision=HIGHEST)
    own_features = feature_table[:atom_count]
    message_table = jnp.dot(feature_table, message_weight, precision=HIGHEST)
    live_mask = (neighbours >= 0).astype(jnp.float32)
    safe_index = jnp.maximum(neighbours, 0)
    neighbour_message = message_table[safe_index] * live_mask[:, :, None]
    offsets = table_pos[:, safe_index] - own_pos[:, :, None]
    distance_sq = lax.optimization_barrier(jnp.sum(offsets * offsets, axis=0))
    distance = jnp.sqrt(distance_sq + SOFTENING)
    direction = offsets / distance
    centres = CENTRE_STEP * jnp.arange(NB, dtype=jnp.float32)
    radial_basis = jnp.exp(-(distance[:, :, None] - centres) ** 2 / (2.0 * CENTRE_STEP ** 2)) * jnp.exp(-0.25 * distance_sq)[:, :, None]
    filters = jnp.einsum('akn,nf->akf', radial_basis, radial_weight, precision=HIGHEST)
    scalar_sum = lax.optimization_barrier(jnp.sum(filters[:, :, :channels] * neighbour_message, axis=1))
    vector_sum = jnp.einsum('xak,akc->xac', direction, filters[:, :, channels:] * neighbour_message, precision=HIGHEST)
    vector_norm = lax.optimization_barrier(jnp.sum(vector_sum * vector_sum, axis=0))
    update = jnp.dot(scalar_sum, scalar_weight, precision=HIGHEST) + jnp.dot(vector_norm, vector_weight, precision=HIGHEST)
    hidden = own_features + jax.nn.silu(update)
    energy = jnp.dot(jax.nn.silu(jnp.dot(hidden, readout_hidden, precision=HIGHEST)), readout_vector, precision=HIGHEST)
    charges = jnp.dot(hidden, charge_weight, precision=HIGHEST)
    return (energy, charges)

def wave_vectors(wave_index, box_first, box_second):
    extent = jnp.array([box_first, box_second, BOX_HEIGHT], dtype=jnp.float32)
    vectors = TWO_PI * wave_index.astype(jnp.float32) / extent[:, None]
    squared = lax.optimization_barrier(jnp.sum(vectors * vectors, axis=0))
    green_weight = jnp.exp(-squared / (4.0 * SPLITTING ** 2)) / squared
    return (vectors, green_weight)

def phases(global_pos, vectors):
    angles = global_pos[0][:, None] * vectors[0] + global_pos[1][:, None] * vectors[1] + global_pos[2][:, None] * vectors[2]
    return (jnp.cos(angles), jnp.sin(angles))

def tables(positions, species, ghost_index):
    domains = N_GX * N_GY
    grid_pos = positions.reshape(3, N_GX, N_GY, A_DEV)
    grid_species = species.reshape(N_GX, N_GY, A_DEV)
    grid_ghost = ghost_index.reshape(N_GX, N_GY, G)
    border_pos = jnp.take_along_axis(grid_pos, jnp.broadcast_to(grid_ghost[None], (3, N_GX, N_GY, G)), axis=3)
    border_species = jnp.take_along_axis(grid_species, grid_ghost, axis=2)
    pos_blocks = [grid_pos]
    species_blocks = [grid_species]
    for row_step in range(3):
        for column_step in range(3):
            rolled = jnp.roll(border_pos, (1 - row_step, 1 - column_step), axis=(1, 2))
            shift_vector = jnp.array([row_step - 1, column_step - 1, 0], dtype=jnp.float32)
            pos_blocks.append(rolled + shift_vector[:, None, None, None])
            species_blocks.append(jnp.roll(border_species, (1 - row_step, 1 - column_step), axis=(0, 1)))
    table_pos = jnp.concatenate(pos_blocks, axis=3).reshape(3, domains, A_DEV + 9 * G).transpose(1, 0, 2)
    table_species = jnp.concatenate(species_blocks, axis=2).reshape(domains, A_DEV + 9 * G)
    return (table_pos, table_species)

def total_energy(positions, species, neighbours, ghost_index, wave_index, embedding, radial_weight, message_weight, scalar_weight, vector_weight, readout_hidden, readout_vector, charge_weight):
    domains = N_GX * N_GY
    table_pos, table_species = tables(positions, species, ghost_index)
    one_hots = (table_species[:, :, None] == jnp.arange(NS, dtype=jnp.int32)).astype(jnp.float32)
    own_pos = positions.reshape(3, domains, A_DEV).transpose(1, 0, 2)
    neighbour_rows = neighbours.reshape(domains, A_DEV, K)

    def one_domain(pieces):
        return short_range(pieces[0], pieces[1], pieces[2], pieces[3], embedding, radial_weight, message_weight, scalar_weight, vector_weight, readout_hidden, readout_vector, charge_weight)
    energies, charges = lax.map(jax.checkpoint(one_domain), (own_pos, table_pos, one_hots, neighbour_rows))
    vectors, green_weight = wave_vectors(wave_index, N_GX, N_GY)
    domain_ids = jnp.arange(domains, dtype=jnp.int32)
    anchors = jnp.stack([(domain_ids // N_GY).astype(jnp.float32), (domain_ids % N_GY).astype(jnp.float32), jnp.zeros((domains,), jnp.float32)], axis=1)
    global_pos = own_pos + anchors[:, :, None]
    mean_charge = lax.optimization_barrier(jnp.sum(charges, axis=(0, 1))) / ATOMS
    neutral = charges - mean_charge

    def add_structure(running, pieces):
        cosines, sine_terms = phases(pieces[0], vectors)
        cos_part = jnp.einsum('aq,ak->qk', pieces[1], cosines, precision=HIGHEST)
        sin_part = jnp.einsum('aq,ak->qk', pieces[1], sine_terms, precision=HIGHEST)
        return ((running[0] + cos_part, running[1] + sin_part), None)
    empty_sum = jnp.zeros((Q, KV), jnp.float32)
    (structure_cos, structure_sin), unused = lax.scan(jax.checkpoint(add_structure), (empty_sum, empty_sum), (global_pos, neutral))
    weighted_cos = green_weight * structure_cos
    weighted_sin = green_weight * structure_sin
    long_energy = jnp.sum(green_weight * lax.optimization_barrier(jnp.sum(structure_cos * structure_cos + structure_sin * structure_sin, axis=0))) / ATOMS

    def site_term(pieces):
        cosines, sine_terms = phases(pieces[0], vectors)
        potential = (jnp.dot(cosines, weighted_cos.T, precision=HIGHEST) + jnp.dot(sine_terms, weighted_sin.T, precision=HIGHEST)) / ATOMS
        return lax.optimization_barrier(jnp.sum(pieces[1] * potential, axis=1))
    site_long = lax.map(jax.checkpoint(site_term), (global_pos, neutral))
    atom_energy = (energies + site_long).reshape(ATOMS)
    return (jnp.sum(energies) + long_energy, atom_energy)

def reference(positions, species, neighbours, ghost_index, wave_index, embedding, radial_weight, message_weight, scalar_weight, vector_weight, readout_hidden, readout_vector, charge_weight):
    gradient, atom_energy = jax.grad(total_energy, has_aux=True)(positions, species, neighbours, ghost_index, wave_index, embedding, radial_weight, message_weight, scalar_weight, vector_weight, readout_hidden, readout_vector, charge_weight)
    return (-gradient, atom_energy)
```

```python
import functools

import jax
import jax.numpy as jnp
from jax import lax
from jax.experimental import pallas as pl
from jax.experimental.pallas import tpu as pltpu
from jax.sharding import PartitionSpec as P

NB = 8
NS = 8
HIGHEST = lax.Precision.HIGHEST
TWO_PI = 6.283185307179586
BOX_HEIGHT = 4.0
SPLITTING = 2.5
SOFTENING = 0.01
CENTRE_STEP = 0.3
AXES = ("gx", "gy")

HX = 9
LZ = 4
NY = 32
XF = 2 * HX - 1
PAIRS = XF * LZ
PROWS = 72
ROWS = 2304
UNIT_ROW = PAIRS * 32
TOTAL_ROW = UNIT_ROW + PROWS
CHUNK = 72

F32 = jnp.float32
BF16 = jnp.bfloat16
NT = (((1,), (1,)), ((), ()))
NN = (((1,), (0,)), ((), ()))


def mm(a, b, dims=NN, precision=None):
    return lax.dot_general(a, b, dims, precision=precision, preferred_element_type=F32)


def parts(x):
    high = x.astype(BF16)
    return high, (x - high.astype(F32)).astype(BF16)


def mm3(a, b, dims=NN):
    a_high, a_low = parts(a)
    b_high, b_low = parts(b)
    return mm(a_high, b_high, dims) + (mm(a_low, b_high, dims) + mm(a_high, b_low, dims))


def cos_turns(t):
    r = t - jnp.floor(t + 0.5)
    s = (0.25 - jnp.abs(r)) * TWO_PI
    q = s * s
    p = -2.5052108e-08 + q * 1.6059044e-10
    p = 2.7557319e-06 + q * p
    p = -1.9841270e-04 + q * p
    p = 8.3333333e-03 + q * p
    p = -1.6666667e-01 + q * p
    return s + s * (q * p)


def silu_parts(x):
    gate = 1.0 / (1.0 + jnp.exp(-x))
    return x * gate, gate * (1.0 + x * (1.0 - gate))


def iota(shape, dim):
    return lax.broadcasted_iota(jnp.int32, shape, dim)


def call(kernel, outs, scratch=(), flops=0, nbytes=0, smem=0, vmem=56, inputs=0):
    specs = None
    if smem:
        specs = [pl.BlockSpec(memory_space=pltpu.SMEM)] * smem + [
            pl.BlockSpec(memory_space=pltpu.VMEM)
        ] * (inputs - smem)
    options = {} if specs is None else {"in_specs": specs}
    return pl.pallas_call(
        kernel,
        out_shape=[jax.ShapeDtypeStruct(s, d) for s, d in outs],
        scratch_shapes=list(scratch),
        compiler_params=pltpu.CompilerParams(vmem_limit_bytes=vmem * 2**20),
        cost_estimate=pl.CostEstimate(flops=flops, bytes_accessed=nbytes, transcendentals=0),
        **options,
    )


def border_kernel(pos_ref, species_ref, ghost_ref, out_ref, tab_ref):
    atoms = pos_ref.shape[1]
    tab_ref[0:3, :] = pos_ref[...]
    tab_ref[3:4, :] = species_ref[...].astype(F32)
    for part in range(ghost_ref.shape[1] // 128):
        lanes = pl.ds(128 * part, 128)
        index = jnp.broadcast_to(ghost_ref[:, lanes], (8, 128))
        high, low = index >> 7, index & 127
        value = jnp.zeros((8, 128), F32)
        for block in range(atoms // 128):
            source = tab_ref[:, pl.ds(128 * block, 128)]
            value = jnp.where(high == block, jnp.take_along_axis(source, low, axis=1), value)
        out_ref[:, lanes] = value[0:4]


def prepare_kernel(
    grid,
    where_ref,
    pos_ref,
    wave_ref,
    nbr_ref,
    radial_ref,
    message_ref,
    scalar_ref,
    vector_ref,
    hidden_ref,
    charge_ref,
    nbr_out,
    xz_out,
    dx_out,
    dz_out,
    y_out,
    ycat_out,
    dycat_out,
    unit_out,
    table_out,
    wide_out,
    narrow_out,
    back_out,
):
    extent_x, extent_y, atoms_all = grid
    atoms = pos_ref.shape[1]
    u, v = where_ref[0], where_ref[1]
    x, y, z = pos_ref[0:1, :], pos_ref[1:2, :], pos_ref[2:3, :]

    row = iota((PROWS, atoms), 0)
    xf, order_z = row >> 2, (row & 3) + 1
    order_x = jnp.where(xf < HX, xf, xf - (HX - 1))
    valid = row < PAIRS
    shift_x = jnp.where(xf < HX, 0.0, 0.25)
    whole_x = lax.rem(order_x * u, extent_x).astype(F32)
    turn_x = (order_x.astype(F32) * x + whole_x) / extent_x - shift_x
    fx = jnp.where(valid, cos_turns(turn_x), 0.0)
    gx = jnp.where(valid, cos_turns(turn_x + 0.25) * order_x.astype(F32) * (TWO_PI / extent_x), 0.0)
    whole_y = lax.rem(v, 2 * extent_y).astype(F32)
    turn_z = order_z.astype(F32) * z * (1.0 / BOX_HEIGHT) - (y + whole_y) * (0.5 / extent_y)
    for half in range(2):
        fz = cos_turns(turn_z - 0.25 * half)
        gz = cos_turns(turn_z - 0.25 * half + 0.25)
        xz_out[half] = fx * fz
        dx_out[half] = gx * fz
        dz_out[half] = fx * gz

    row = iota((2 * NY, atoms), 0)
    twice = 2 * (row & (NY - 1)) + 1
    shift_y = jnp.where(row < NY, 0.0, 0.25)
    whole = lax.rem(twice * v, 2 * extent_y).astype(F32)
    turn_y = (twice.astype(F32) * y + whole) * (0.5 / extent_y) - shift_y
    fy = cos_turns(turn_y)
    gy = cos_turns(turn_y + 0.25) * twice.astype(F32) * (0.5 * TWO_PI / extent_y)
    y_out[...] = fy
    high, low = parts(fy)
    ycat_out[0 : 2 * NY, :] = high
    ycat_out[2 * NY :, :] = low
    high, low = parts(gy)
    dycat_out[0 : 2 * NY, :] = high
    dycat_out[2 * NY :, :] = low

    both = jnp.concatenate([fy, fy], axis=0)
    first = mm(xz_out[0], both, NT, HIGHEST)
    second = mm(xz_out[1], both, NT, HIGHEST)
    lane = iota((PROWS, 128), 1)
    unit_out[...] = jnp.where(lane < 64, first, second)

    step = wave_ref.shape[1]
    order = iota((40, step), 0)
    along_x, along_y, along_z = wave_ref[0:1, :], wave_ref[1:2, :], wave_ref[2:3, :]
    matches_z = ((order & 3) + 1 == along_z) & (order < HX * LZ)
    plus = matches_z & ((order >> 2) == along_x)
    minus = matches_z & ((order >> 2) == -along_x) & (order >= LZ)
    lanes = iota((128, step), 0) & (NY - 1)
    up = (lanes == along_y).astype(F32).astype(BF16)
    down = (-lanes - 1 == along_y).astype(F32).astype(BF16)
    plus = plus.astype(F32).astype(BF16)
    minus = minus.astype(F32).astype(BF16)
    order = iota((40, 128), 0)
    lanes = iota((40, 128), 1)
    wave_b = (lanes & (NY - 1)).astype(F32)
    kx = (order >> 2).astype(F32) * (TWO_PI / extent_x)
    kz = ((order & 3) + 1).astype(F32) * (TWO_PI / BOX_HEIGHT)

    def weights(ky):
        squared = kx * kx + ky * ky + kz * kz
        return jnp.exp(-squared / (4.0 * SPLITTING**2)) / squared / atoms_all

    green_up = weights(wave_b * (TWO_PI / extent_y))
    green_down = weights((wave_b + 1.0) * (TWO_PI / extent_y))
    pp = green_up * mm(plus, up, NT)
    pm = green_down * mm(plus, down, NT)
    mp = green_up * mm(minus, up, NT)
    mn = green_down * mm(minus, down, NT)
    quarter = lanes >> 5
    sign_t = jnp.where((quarter == 1) | (quarter == 2), 1.0, -1.0)
    sign_st = jnp.where((quarter & 1) == 1, 1.0, -1.0)
    sign_s = jnp.where(quarter >= 2, 1.0, -1.0)
    table_out[0] = (pp + pm) + (mp + mn)
    table_out[1] = sign_t * ((pp - pm) + (mp - mn))
    table_out[2] = sign_st * ((pp - pm) - (mp - mn))
    table_out[3] = sign_s * ((pp + pm) - (mp + mn))

    col = iota((NB, 512), 1)
    sub = iota((NB, 512), 0)
    pick_b = ((col >> 6) == sub).astype(F32)
    pick_s = (((col >> 3) & 7) == sub).astype(F32)
    message = message_ref[...]
    spread = mm(message, pick_s, NN, HIGHEST)
    channels = message.shape[0]
    for which in range(2):
        wide = mm(radial_ref[which * channels : (which + 1) * channels, :], pick_b, NN, HIGHEST) * spread
        high, low = parts(wide)
        wide_out[which, 0:channels] = high
        wide_out[which, channels:] = low
    col = iota((NB, 64), 1)
    sub = iota((NB, 64), 0)
    pick_b = ((col >> 3) == sub).astype(F32)
    pick_s = ((col & 7) == sub).astype(F32)
    spread = mm(message, pick_s, NN, HIGHEST)
    for which in range(2):
        narrow = mm(radial_ref[which * channels : (which + 1) * channels, :], pick_b, NN, HIGHEST) * spread
        narrow_out[which] = narrow.T
    back_out[0] = scalar_ref[...].T
    back_out[1] = vector_ref[...].T
    back_out[2] = hidden_ref[...].T
    back_out[3, 0:32] = charge_ref[...].T
    nbr_out[...] = nbr_ref[...].T


def basis_terms(dist, rho, live):
    envelope = jnp.exp(-0.25 * rho) * live
    out = []
    for b in range(NB):
        off = dist - CENTRE_STEP * b
        out.append((jnp.exp(off * off * (-0.5 / CENTRE_STEP**2)) * envelope, off))
    return out


def forward_kernel(
    where_ref,
    pos_ref,
    species_ref,
    mid_ref,
    prev_ref,
    next_ref,
    nbr_ref,
    embed_ref,
    wide_ref,
    back_ref,
    hidden_ref,
    readout_ref,
    xz_ref,
    ycat_ref,
    unit_ref,
    energy_out,
    charge_out,
    hbar_out,
    slope_out,
    vsum_out,
    geo_out,
    keep_out,
    send_out,
    tab_ref,
    moment_ref,
    qh_ref,
    ql_ref,
    pay_ref,
):
    atoms = pos_ref.shape[1]
    tiles = atoms // 128
    for c in range(3):
        for j in range(tiles):
            tab_ref[c, j : j + 1, :] = pos_ref[c : c + 1, pl.ds(128 * j, 128)]
    for j in range(tiles):
        tab_ref[3, j : j + 1, :] = species_ref[:, pl.ds(128 * j, 128)].astype(F32)
    for i in range(3):
        for j, block_ref in enumerate((prev_ref, mid_ref, next_ref)):
            block = block_ref[i]
            shifts = (i - 1.0, j - 1.0, 0.0, 0.0)
            for c in range(4):
                for h in range(2):
                    at = tiles + 2 * (3 * i + j) + h
                    tab_ref[c, at : at + 1, :] = block[c : c + 1, 128 * h : 128 * h + 128] + shifts[c]

    def lane_tile(t, carry):
        lanes = pl.ds(pl.multiple_of(t * 128, 128), 128)
        for tile in range(4):
            index = nbr_ref[pl.ds(8 * tile, 8), lanes]
            live = (index >= 0).astype(F32)
            index = jnp.maximum(index, 0)
            high, low = index >> 7, index & 127
            value = [jnp.zeros((8, 128), F32) for _ in range(4)]
            for block in range(tiles + 18):
                if block // 2 == tiles // 2 + 4:
                    continue
                here = high == block
                for c in range(4):
                    source = jnp.broadcast_to(tab_ref[c, block : block + 1, :], (8, 128))
                    value[c] = jnp.where(here, jnp.take_along_axis(source, low, axis=1), value[c])
            rx, ry, rz = (value[c] - pos_ref[c : c + 1, lanes] for c in range(3))
            rho = rx * rx + ry * ry + rz * rz
            dist = jnp.sqrt(rho + SOFTENING)
            inv = 1.0 / dist
            rows = pl.ds(8 * tile, 8)
            geo_out[0, rows, lanes] = rx * inv
            geo_out[1, rows, lanes] = ry * inv
            geo_out[2, rows, lanes] = rz * inv
            geo_out[3, rows, lanes] = dist
            geo_out[4, rows, lanes] = rho
            geo_out[5, rows, lanes] = value[3]
            geo_out[6, rows, lanes] = live
        dist = geo_out[3, :, lanes]
        terms = basis_terms(dist, geo_out[4, :, lanes], geo_out[6, :, lanes])
        kind = geo_out[5, :, lanes]
        for f in range(4):
            for b in range(NB):
                value = terms[b][0] if f == 0 else terms[b][0] * geo_out[f - 1, :, lanes]
                for s in range(NS):
                    chosen = jnp.where(kind == float(s), value, 0.0)
                    total = (chosen[0:8] + chosen[8:16]) + (chosen[16:24] + chosen[24:32])
                    moment_ref[f, pl.ds(8 * (8 * b + s), 8), lanes] = total
        return carry

    lax.fori_loop(0, tiles, lane_tile, 0)

    def gathered(f):
        wide = wide_ref[0 if f == 0 else 1]
        high, low = parts(moment_ref[f])
        both = mm(wide, high)
        return both[0:128] + both[128:256] + mm(wide[0:128], low)

    scalar_sum = gathered(0)
    norm = None
    for c in range(3):
        vector = gathered(c + 1)
        vsum_out[c] = vector
        norm = vector * vector if norm is None else norm + vector * vector
    update = mm3(back_ref[0], scalar_sum) + mm3(back_ref[1], norm)
    feature = jnp.zeros_like(update)
    kinds = species_ref[...]
    for s in range(NS):
        feature = jnp.where(kinds == s, embed_ref[:, s : s + 1], feature)
    act, slope = silu_parts(update)
    slope_out[...] = slope
    hidden = feature + act
    act, slope = silu_parts(mm3(back_ref[2], hidden))
    readout = readout_ref[...]
    energy_out[...] = jnp.sum(act * readout, axis=0, keepdims=True)
    hbar_out[...] = mm3(hidden_ref[...], slope * readout)
    charges = mm3(back_ref[3, 0:32], hidden)
    charge_out[...] = charges

    total = jnp.sum(charges, axis=1, keepdims=True)
    local = total * (1.0 / atoms)
    centred = charges - local
    lane = iota((32, 128), 1)
    group = 17

    def sums(k, carry):
        for half in range(2):
            for i in range(group):
                row = xz_ref[half, pl.ds(k * group + i, 1), :]
                high, low = parts(centred * row)
                qh_ref[half, 32 * i : 32 * i + 32, :] = high
                ql_ref[half, 32 * i : 32 * i + 32, :] = low
        ycat = ycat_ref[...]
        first = mm(qh_ref[0], ycat, NT) + mm(ql_ref[0], ycat, NT)
        second = mm(qh_ref[1], ycat, NT) + mm(ql_ref[1], ycat, NT)
        first = first + pltpu.roll(first, 64, 1)
        second = second + pltpu.roll(second, 64, 1)
        for i in range(group):
            rows = slice(32 * i, 32 * i + 32)
            packed = jnp.where(lane < 64, first[rows], second[rows])
            packed = packed + local * unit_ref[pl.ds(k * group + i, 1), :]
            at = pl.multiple_of((k * group + i) * 32, 32)
            pay_ref[pl.ds(at, 32), :] = packed
        return carry

    lax.fori_loop(0, PAIRS // group, sums, 0)
    pay_ref[UNIT_ROW:TOTAL_ROW, :] = unit_ref[...]
    pay_ref[TOTAL_ROW : TOTAL_ROW + 32, :] = jnp.broadcast_to(total, (32, 128))
    pay_ref[TOTAL_ROW + 32 :, :] = jnp.zeros((ROWS - TOTAL_ROW - 32, 128), F32)
    place(where_ref, pay_ref, keep_out, send_out, False)


def place(where_ref, whole_ref, near_ref, far_ref, inward):
    for c in range(2):
        for y in range(4):
            for x in range(4):
                absolute = ((where_ref[2] + c) & 1) * 16 + ((where_ref[3] + y) & 3) * 4 + ((where_ref[4] + x) & 3)
                there = pl.ds(pl.multiple_of(absolute * CHUNK, 8), CHUNK)
                here = pl.ds((4 * y + x) * CHUNK, CHUNK)
                part = near_ref if c == 0 else far_ref
                if inward:
                    whole_ref[there, :] = part[here, :]
                else:
                    part[here, :] = whole_ref[there, :]


def quarters(x, which):
    lane = iota(x.shape, 1)
    if which == 2:
        return pltpu.roll(x, 64, 1)
    even = ((lane >> 5) & 1) == 0
    if which == 1:
        return jnp.where(even, pltpu.roll(x, 96, 1), pltpu.roll(x, 32, 1))
    return jnp.where(even, pltpu.roll(x, 32, 1), pltpu.roll(x, 96, 1))


def backward_kernel(
    atoms_all,
    where_ref,
    near_ref,
    far_ref,
    table_ref,
    xz_ref,
    ycat_ref,
    energy_ref,
    charge_ref,
    hbar_ref,
    slope_ref,
    vsum_ref,
    geo_ref,
    nbr_ref,
    scalar_ref,
    vector_ref,
    weight_ref,
    narrow_ref,
    site_out,
    neutral_out,
    va_out,
    vb_out,
    own_out,
    prev_out,
    mid_out,
    next_out,
    sum_ref,
    ta_ref,
    tb_ref,
    g_ref,
    rbar_ref,
):
    atoms = nbr_ref.shape[1]
    tiles = atoms // 128
    place(where_ref, sum_ref, near_ref, far_ref, True)
    mean = sum_ref[TOTAL_ROW : TOTAL_ROW + 32, :] * (1.0 / atoms_all)
    lane = iota((32, 128), 1)

    def put(p, value):
        high = value.astype(BF16).astype(F32)
        low = value - high
        rows = pl.ds(pl.multiple_of(p * 32, 32), 32)
        va_out[rows, :] = jnp.where(lane < 64, high, pltpu.roll(low, 64, 1)).astype(BF16)
        vb_out[rows, :] = jnp.where(lane < 64, pltpu.roll(high, 64, 1), low).astype(BF16)

    def tile_of(p):
        unit = sum_ref[pl.ds(UNIT_ROW + p, 1), :]
        return sum_ref[pl.ds(pl.multiple_of(p * 32, 32), 32), :] - mean * unit, unit

    overlap = jnp.zeros((32, 128), F32)
    for l in range(LZ):
        cos_tile, unit = tile_of(l)
        g0 = table_ref[0, l : l + 1, :]
        gt = table_ref[1, l : l + 1, :]
        value = g0 * cos_tile + gt * quarters(cos_tile, 3)
        overlap = overlap + value * unit
        put(l, value)

    def mix(a, overlap):
        for l in range(LZ):
            at = a * LZ + l
            sat = (a + HX - 1) * LZ + l
            cos_tile, cos_unit = tile_of(at)
            sin_tile, sin_unit = tile_of(sat)
            g0 = table_ref[0, pl.ds(at, 1), :]
            gt = table_ref[1, pl.ds(at, 1), :]
            gst = table_ref[2, pl.ds(at, 1), :]
            gs = table_ref[3, pl.ds(at, 1), :]
            value = (g0 * cos_tile + gt * quarters(cos_tile, 3)) + (
                gst * quarters(sin_tile, 1) + gs * quarters(sin_tile, 2)
            )
            overlap = overlap + value * cos_unit
            put(at, value)
            value = (g0 * sin_tile + gt * quarters(sin_tile, 3)) - (
                gst * quarters(cos_tile, 1) + gs * quarters(cos_tile, 2)
            )
            overlap = overlap + value * sin_unit
            put(sat, value)
        return overlap

    overlap = lax.fori_loop(1, HX, mix, overlap)
    potential_mean = jnp.sum(overlap, axis=1, keepdims=True) * (1.0 / atoms_all)

    high, low = ycat_ref[0:64, :], ycat_ref[64:128, :]
    right = jnp.concatenate([high, high, low, low], axis=0)
    group = 17

    def evaluate(k, potential):
        rows = pl.ds(pl.multiple_of(k * group * 32, 32), group * 32)
        left = va_out[rows, :]
        ta_ref[...] = mm(jnp.concatenate([left, left], axis=1), right)
        left = vb_out[rows, :]
        tb_ref[...] = mm(jnp.concatenate([left, left], axis=1), right)
        for i in range(group):
            first = xz_ref[0, pl.ds(k * group + i, 1), :]
            second = xz_ref[1, pl.ds(k * group + i, 1), :]
            here = slice(32 * i, 32 * i + 32)
            potential = potential + (first * ta_ref[here, :] + second * tb_ref[here, :])
        return potential

    potential = lax.fori_loop(0, PAIRS // group, evaluate, jnp.zeros((32, atoms), F32))
    neutral = charge_ref[...] - mean[:, 0:1]
    neutral_out[...] = neutral
    site_out[...] = energy_ref[...] + jnp.sum(neutral * potential, axis=0, keepdims=True)
    charge_bar = 2.0 * (potential - potential_mean)
    update_bar = (hbar_ref[...] + mm3(weight_ref[...], charge_bar)) * slope_ref[...]
    scalar_bar = mm3(scalar_ref[...], update_bar)
    norm_bar = 2.0 * mm3(vector_ref[...], update_bar)
    g_ref[0] = mm3(narrow_ref[0], scalar_bar)
    for c in range(3):
        g_ref[c + 1] = mm3(narrow_ref[1], vsum_ref[c] * norm_bar)

    def slots(t, carry):
        lanes = pl.ds(pl.multiple_of(t * 128, 128), 128)
        own = [jnp.zeros((8, 128), F32) for _ in range(3)]
        for tile in range(4):
            rows = pl.ds(8 * tile, 8)
            unit = [geo_ref[c, rows, lanes] for c in range(3)]
            dist = geo_ref[3, rows, lanes]
            kind = geo_ref[5, rows, lanes].astype(jnp.int32)
            terms = basis_terms(dist, geo_ref[4, rows, lanes], geo_ref[6, rows, lanes])
            inv = 1.0 / dist
            ubar = [jnp.zeros((8, 128), F32) for _ in range(3)]
            plain = jnp.zeros((8, 128), F32)
            tilted = jnp.zeros((8, 128), F32)
            for b in range(NB):
                value, off = terms[b]
                picked = [
                    jnp.take_along_axis(g_ref[f, 8 * b : 8 * b + 8, lanes], kind, axis=0) for f in range(4)
                ]
                bar = picked[0]
                for c in range(3):
                    bar = bar + unit[c] * picked[c + 1]
                    ubar[c] = ubar[c] + value * picked[c + 1]
                bar = bar * value
                plain = plain + bar
                tilted = tilted + bar * off
            along = ubar[0] * unit[0] + ubar[1] * unit[1] + ubar[2] * unit[2]
            dist_bar = tilted * (-1.0 / CENTRE_STEP**2) - along * inv
            radial = dist * (2.0 * (-0.25 * plain) + dist_bar * inv)
            for c in range(3):
                bar = ubar[c] * inv + unit[c] * radial
                rbar_ref[c, rows, lanes] = bar
                own[c] = own[c] + bar
        for c in range(3):
            own_out[c : c + 1, lanes] = -jnp.sum(own[c], axis=0, keepdims=True)
        return carry

    lax.fori_loop(0, tiles, slots, 0)

    block_rows = 24
    rows_high = iota((block_rows, atoms), 0)
    rows_low = iota((128, atoms), 0)

    def scatter(s, total):
        index = jnp.maximum(nbr_ref[pl.ds(s, 1), :], 0)
        at_high = rows_high == (index >> 7)
        at_low = jnp.where(rows_low == (index & 127), 1.0, 0.0).astype(BF16)
        pieces = []
        for c in range(3):
            value = rbar_ref[c, pl.ds(s, 1), :]
            high = value.astype(BF16).astype(F32)
            pieces.append(jnp.where(at_high, high, 0.0))
            pieces.append(jnp.where(at_high, value - high, 0.0))
        left = jnp.concatenate(pieces, axis=0).astype(BF16)
        return total + mm(left, at_low, NT)

    total = lax.fori_loop(0, nbr_ref.shape[0], scatter, jnp.zeros((6 * block_rows, 128), F32))
    for c in range(3):
        at = 2 * block_rows * c
        table = total[at : at + block_rows] + total[at + block_rows : at + 2 * block_rows]
        for j in range(tiles):
            lanes = pl.ds(128 * j, 128)
            own_out[c : c + 1, lanes] = own_out[c : c + 1, lanes] + table[j : j + 1]
        for i in range(3):
            for j, out in enumerate((prev_out, mid_out, next_out)):
                for h in range(2):
                    row = tiles + 2 * (3 * i + j) + h
                    out[i, c : c + 1, 128 * h : 128 * h + 128] = table[row : row + 1]


def ewald_kernel(
    grid,
    va_ref,
    vb_ref,
    xz_ref,
    dx_ref,
    dz_ref,
    ycat_ref,
    dycat_ref,
    neutral_ref,
    own_ref,
    out_ref,
    ta_ref,
    tb_ref,
    da_ref,
    db_ref,
):
    extent_y = grid
    atoms = neutral_ref.shape[1]
    right = [
        jnp.concatenate([ref[0:64, :], ref[0:64, :], ref[64:128, :], ref[64:128, :]], axis=0)
        for ref in (ycat_ref, dycat_ref)
    ]
    neutral = neutral_ref[...]
    group = 17

    def step(k, sums):
        rows = pl.ds(pl.multiple_of(k * group * 32, 32), group * 32)
        for ref, even, odd in ((va_ref, ta_ref, da_ref), (vb_ref, tb_ref, db_ref)):
            left = ref[rows, :]
            left = jnp.concatenate([left, left], axis=1)
            even[...] = mm(left, right[0])
            odd[...] = mm(left, right[1])
        sum_x, sum_y, sum_z = sums
        for i in range(group):
            at = k * group + i
            order = (lax.rem(at, LZ) + 1).astype(F32) * (TWO_PI / BOX_HEIGHT)
            here = slice(32 * i, 32 * i + 32)
            for half, even, odd in ((0, ta_ref, da_ref), (1, tb_ref, db_ref)):
                value = even[here, :]
                sum_x = sum_x + dx_ref[half, pl.ds(at, 1), :] * value
                turned = dz_ref[half, pl.ds(at, 1), :]
                sum_z = sum_z + (order * turned) * value
                sum_y = sum_y + (
                    xz_ref[half, pl.ds(at, 1), :] * odd[here, :]
                    - ((0.5 * TWO_PI / extent_y) * turned) * value
                )
        return sum_x, sum_y, sum_z

    zero = jnp.zeros((32, atoms), F32)
    sums = lax.fori_loop(0, PAIRS // group, step, (zero, zero, zero))
    for c in range(3):
        out_ref[c : c + 1, :] = own_ref[c : c + 1, :] + 2.0 * jnp.sum(neutral * sums[c], axis=0, keepdims=True)


def finish_kernel(base_ref, mid_ref, first_ref, second_ref, ghost_ref, out_ref):
    atoms = base_ref.shape[1]
    returned = mid_ref[...] + first_ref[...] + second_ref[...]
    high = returned.astype(BF16).astype(F32)
    rest = returned - high
    middle = rest.astype(BF16).astype(F32)
    split = jnp.concatenate([high, middle, rest - middle, jnp.zeros((7, 256), F32)], axis=0).astype(BF16)
    at = jnp.where(iota((atoms, 256), 0) == ghost_ref[...], 1.0, 0.0).astype(BF16)
    spread = mm(split, at, NT)
    out_ref[...] = -(base_ref[...] + ((spread[0:3] + spread[3:6]) + spread[6:9]))


def add_kernel(count, *refs):
    ins, outs = refs[:count], refs[count:]
    rows = outs[0].shape[0]
    for k, out in enumerate(outs):
        here = pl.ds(k * rows, rows)
        total = ins[0][here, :]
        for ref in ins[1:]:
            total = total + ref[here, :]
        out[...] = total


def add_up(arrays, pieces):
    rows = arrays[0].shape[0] // pieces
    return call(functools.partial(add_kernel, len(arrays)), [((rows, 128), F32)] * pieces)(*arrays)


def shifted(array, axis, by):
    devices = lax.axis_size(axis)
    return lax.ppermute(array, axis, [(i, (i + by) % devices) for i in range(devices)])


class Ring:
    def __init__(self):
        self.first, self.second = lax.axis_size("gx"), lax.axis_size("gy")
        u, v = lax.axis_index("gx"), lax.axis_index("gy")
        self.index = [u, v, u % 2, v % 4, v // 4 % 4]

    def move(self, array, axis, by):
        pairs = []
        for device in range(self.first * self.second):
            u, v = divmod(device, self.second)
            core, z, y, x, top = u % 2, u // 2, v % 4, v // 4 % 4, v // 16
            if axis == "core":
                core = (core + by) % 2
            elif axis == "y":
                y = (y + by) % 4
            elif axis == "x":
                x = (x + by) % 4
            elif axis == "z":
                z = (z + by) % 4
            elif axis == "top":
                top = (top + by) % 2
            pairs.append((device, (z * 2 + core) * self.second + top * 16 + x * 4 + y))
        return lax.ppermute(array, AXES, pairs)


def total_over_devices(ring, keep, send):
    got = ring.move(send, "core", 1)
    for axis in ("y", "x"):
        parts_ = add_up([keep, got] if axis == "y" else [keep] + got, 4)
        keep = parts_[0]
        got = [ring.move(parts_[d], axis, d) for d in range(1, 4)]
    (keep,) = add_up([keep] + got, 1)
    got = [ring.move(keep, "z", d) for d in range(1, 4)]
    (keep,) = add_up([keep] + got, 1)
    (keep,) = add_up([keep, ring.move(keep, "top", 1)], 1)
    for axis in ("x", "y"):
        keep = jnp.concatenate([keep] + [ring.move(keep, axis, -d) for d in range(1, 4)], axis=0)
    return keep, ring.move(keep, "core", 1)


def shards(
    positions,
    species,
    neighbours,
    ghost_index,
    wave_index,
    embedding,
    radial_weight,
    message_weight,
    scalar_weight,
    vector_weight,
    readout_hidden,
    readout_vector,
    charge_weight,
):
    atoms = positions.shape[1]
    ring = Ring()
    atoms_all = atoms * ring.first * ring.second
    where = jnp.stack(ring.index).astype(jnp.int32)
    kinds = species[None]
    ghosts = ghost_index[None]

    (border,) = call(border_kernel, [((4, 256), F32)], [pltpu.VMEM((8, atoms), F32)])(positions, kinds, ghosts)
    mid = jnp.stack([shifted(border, "gx", 1), border, shifted(border, "gx", -1)])
    prev, after = shifted(mid, "gy", 1), shifted(mid, "gy", -1)

    embed_t = embedding.T
    message_t = lax.dot_general(message_weight, embedding, (((0,), (1,)), ((), ())), precision=HIGHEST)
    nbr, xz, dx, dz, _, ycat, dycat, unit, table, wide, narrow, back = call(
        functools.partial(prepare_kernel, (ring.first, ring.second, atoms_all)),
        [
            ((32, atoms), jnp.int32),
            ((2, PROWS, atoms), F32),
            ((2, PROWS, atoms), F32),
            ((2, PROWS, atoms), F32),
            ((64, atoms), F32),
            ((128, atoms), BF16),
            ((128, atoms), BF16),
            ((PROWS, 128), F32),
            ((4, 40, 128), F32),
            ((2, 256, 512), BF16),
            ((2, 64, 128), F32),
            ((4, 128, 128), F32),
        ],
        smem=1,
        inputs=10,
        flops=10**9,
        nbytes=4 * 10**6,
    )(
        where,
        positions,
        wave_index,
        neighbours,
        radial_weight.T,
        message_t,
        scalar_weight,
        vector_weight,
        readout_hidden,
        charge_weight,
    )

    energy, charge, hbar, slope, vsum, geo, keep, send = call(
        forward_kernel,
        [
            ((1, atoms), F32),
            ((32, atoms), F32),
            ((128, atoms), F32),
            ((128, atoms), F32),
            ((3, 128, atoms), F32),
            ((7, 32, atoms), F32),
            ((ROWS // 2, 128), F32),
            ((ROWS // 2, 128), F32),
        ],
        [
            pltpu.VMEM((4, 24, 128), F32),
            pltpu.VMEM((4, 512, atoms), F32),
            pltpu.VMEM((2, 544, atoms), BF16),
            pltpu.VMEM((2, 544, atoms), BF16),
            pltpu.VMEM((ROWS, 128), F32),
        ],
        smem=1,
        inputs=15,
        flops=5 * 10**9,
        nbytes=4 * 10**6,
    )(
        where,
        positions,
        kinds,
        mid,
        prev,
        after,
        nbr,
        embed_t,
        wide,
        back,
        readout_hidden,
        readout_vector[:, None],
        xz,
        ycat,
        unit,
    )

    near, far = total_over_devices(ring, keep, send)

    site, neutral, va, vb, own, g_prev, g_mid, g_next = call(
        functools.partial(backward_kernel, atoms_all),
        [
            ((1, atoms), F32),
            ((32, atoms), F32),
            ((UNIT_ROW, 128), BF16),
            ((UNIT_ROW, 128), BF16),
            ((3, atoms), F32),
            ((3, 3, 256), F32),
            ((3, 3, 256), F32),
            ((3, 3, 256), F32),
        ],
        [
            pltpu.VMEM((ROWS, 128), F32),
            pltpu.VMEM((544, atoms), F32),
            pltpu.VMEM((544, atoms), F32),
            pltpu.VMEM((4, 64, atoms), F32),
            pltpu.VMEM((3, 32, atoms), F32),
        ],
        smem=1,
        inputs=17,
        flops=5 * 10**9,
        nbytes=4 * 10**6,
    )(
        where,
        near,
        far,
        table,
        xz,
        ycat,
        energy,
        charge,
        hbar,
        slope,
        vsum,
        geo,
        nbr,
        scalar_weight,
        vector_weight,
        charge_weight,
        narrow,
    )

    column = g_mid + shifted(g_prev, "gy", -1) + shifted(g_next, "gy", 1)
    first, second = shifted(column[0], "gx", -1), shifted(column[2], "gx", 1)
    (base,) = call(
        functools.partial(ewald_kernel, ring.second),
        [((3, atoms), F32)],
        [pltpu.VMEM((544, atoms), F32)] * 4,
        flops=5 * 10**9,
        nbytes=4 * 10**6,
    )(va, vb, xz, dx, dz, ycat, dycat, neutral, own)
    (forces,) = call(finish_kernel, [((3, atoms), F32)])(base, column[1], first, second, ghosts)
    return forces, site[0]


def solution(mesh):
    return jax.shard_map(
        shards,
        mesh=mesh,
        in_specs=(
            P(None, ("gx", "gy")),
            P(("gx", "gy")),
            P(("gx", "gy"), None),
            P(("gx", "gy")),
            P(),
            P(),
            P(),
            P(),
            P(),
            P(),
            P(),
            P(),
            P(),
        ),
        out_specs=(P(None, ("gx", "gy")), P(("gx", "gy"))),
        check_vma=False,
    )
```

```python
import functools

import jax
import jax.numpy as jnp
from jax import lax
from jax.experimental import pallas as pl
from jax.experimental.pallas import tpu as pltpu
from jax.sharding import PartitionSpec as P

NB = 8
NS = 8
HIGHEST = lax.Precision.HIGHEST
TWO_PI = 6.283185307179586
BOX_HEIGHT = 4.0
SPLITTING = 2.5
SOFTENING = 0.01
CENTRE_STEP = 0.3
AXES = ("gx", "gy")

HX = 9
LZ = 4
NY = 32
XF = 2 * HX - 1
XROWS = 24
SLAB = XF * 32
UNIT_ROW = LZ * SLAB
TOTAL_ROW = UNIT_ROW + LZ * XROWS
ROWS = TOTAL_ROW + 32

F32 = jnp.float32
BF16 = jnp.bfloat16
NT = (((1,), (1,)), ((), ()))
NN = (((1,), (0,)), ((), ()))


def mm(a, b, dims=NN, precision=None):
    return lax.dot_general(a, b, dims, precision=precision, preferred_element_type=F32)


def parts(x):
    high = x.astype(BF16)
    return high, (x - high.astype(F32)).astype(BF16)


def mm3(a, b, dims=NN):
    a_high, a_low = parts(a)
    b_high, b_low = parts(b)
    return mm(a_high, b_high, dims) + (mm(a_low, b_high, dims) + mm(a_high, b_low, dims))


def cos_turns(t):
    r = t - jnp.floor(t + 0.5)
    s = (0.25 - jnp.abs(r)) * TWO_PI
    q = s * s
    p = -2.5052108e-08 + q * 1.6059044e-10
    p = 2.7557319e-06 + q * p
    p = -1.9841270e-04 + q * p
    p = 8.3333333e-03 + q * p
    p = -1.6666667e-01 + q * p
    return s + s * (q * p)


def silu_parts(x):
    gate = 1.0 / (1.0 + jnp.exp(-x))
    return x * gate, gate * (1.0 + x * (1.0 - gate))


def iota(shape, dim):
    return lax.broadcasted_iota(jnp.int32, shape, dim)


def call(kernel, outs, scratch=(), spaces="", flops=0, nbytes=0, vmem=56):
    known = {"s": pltpu.SMEM, "v": pltpu.VMEM, "a": pl.ANY, "h": pltpu.HBM}
    return pl.pallas_call(
        kernel,
        in_specs=[pl.BlockSpec(memory_space=known[letter]) for letter in spaces],
        out_shape=[jax.ShapeDtypeStruct(s, d) for s, d in outs],
        scratch_shapes=list(scratch),
        compiler_params=pltpu.CompilerParams(vmem_limit_bytes=vmem * 2**20),
        cost_estimate=pl.CostEstimate(flops=flops, bytes_accessed=nbytes, transcendentals=0),
    )


def border_kernel(pos_ref, species_ref, ghost_ref, out_ref, tab_ref):
    atoms = pos_ref.shape[1]
    tab_ref[0:3, :] = pos_ref[...]
    tab_ref[3:4, :] = species_ref[...].astype(F32)
    for part in range(ghost_ref.shape[1] // 128):
        lanes = pl.ds(128 * part, 128)
        index = jnp.broadcast_to(ghost_ref[:, lanes], (8, 128))
        high, low = index >> 7, index & 127
        value = jnp.zeros((8, 128), F32)
        for block in range(atoms // 128):
            source = tab_ref[:, pl.ds(128 * block, 128)]
            value = jnp.where(high == block, jnp.take_along_axis(source, low, axis=1), value)
        out_ref[:, lanes] = value[0:4]


def waves(grid, where_ref, pos_ref):
    extent_x, extent_y = grid
    atoms = pos_ref.shape[1]
    u, v = where_ref[0], where_ref[1]
    x, y, z = pos_ref[0:1, :], pos_ref[1:2, :], pos_ref[2:3, :]

    row = iota((XROWS, atoms), 0)
    order = jnp.where(row < HX, row, row - (HX - 1))
    whole = lax.rem(order * u, extent_x).astype(F32)
    order = order.astype(F32)
    turn_x = (order * x + whole) / extent_x - jnp.where(row < HX, 0.0, 0.25)
    rate_x = jnp.where(row < XF, order * (TWO_PI / extent_x), 0.0)

    row = iota((2 * LZ, atoms), 0)
    whole = lax.rem(v, 2 * extent_y).astype(F32)
    turn_z = ((row >> 1) + 1).astype(F32) * z * (1.0 / BOX_HEIGHT) - (y + whole) * (0.5 / extent_y)
    turn_z = turn_z - 0.25 * (row & 1).astype(F32)

    row = iota((2 * NY, atoms), 0)
    twice = 2 * (row & (NY - 1)) + 1
    whole = lax.rem(twice * v, 2 * extent_y).astype(F32)
    twice = twice.astype(F32)
    turn_y = (twice * y + whole) * (0.5 / extent_y) - jnp.where(row < NY, 0.0, 0.25)
    return turn_x, rate_x, turn_z, turn_y, twice * (0.5 * TWO_PI / extent_y)


def prepare_kernel(
    grid,
    where_ref,
    pos_ref,
    embed_ref,
    radial_ref,
    message_ref,
    x_out,
    zy_out,
    unit_out,
    wide_out,
    embed_out,
    message_out,
):
    turn_x, _, turn_z, turn_y, _ = waves(grid, where_ref, pos_ref)
    fx = jnp.where(iota(turn_x.shape, 0) < XF, cos_turns(turn_x), 0.0)
    fz, fy = cos_turns(turn_z), cos_turns(turn_y)
    x_out[...] = fx

    for l in range(LZ):
        zy = jnp.concatenate([fz[2 * l : 2 * l + 1] * fy, fz[2 * l + 1 : 2 * l + 2] * fy], axis=0)
        high, low = parts(zy)
        zy_out[0, 128 * l : 128 * l + 128] = high
        zy_out[1, 128 * l : 128 * l + 128] = low
        unit_out[l] = mm(fx, zy, NT, HIGHEST)

    embed = embed_ref[...].T
    message = mm(message_ref[...].T, embed, NN, HIGHEST)
    embed_out[...] = embed
    message_out[...] = message
    col = iota((NB, 512), 1)
    sub = iota((NB, 512), 0)
    pick_b = ((col >> 6) == sub).astype(F32)
    pick_s = (((col >> 3) & 7) == sub).astype(F32)
    spread = mm(message, pick_s, NN, HIGHEST)
    radial = radial_ref[...].T
    channels = message.shape[0]
    for which in range(2):
        wide = mm(radial[which * channels : (which + 1) * channels], pick_b, NN, HIGHEST) * spread
        high, low = parts(wide)
        wide_out[which, 0:channels] = high
        wide_out[which, channels:] = low


def later_kernel(
    grid,
    atoms_all,
    where_ref,
    pos_ref,
    wave_ref,
    radial_ref,
    message_ref,
    charge_ref,
    table_out,
    narrow_out,
    charge_out,
    dx_out,
    z_out,
    dz_out,
    y_out,
    dy_out,
):
    extent_x, extent_y = grid
    turn_x, rate_x, turn_z, turn_y, rate_y = waves(grid, where_ref, pos_ref)
    dx_out[...] = cos_turns(turn_x + 0.25) * rate_x
    z_out[...] = cos_turns(turn_z)
    dz_out[...] = cos_turns(turn_z + 0.25)
    y_out[...] = cos_turns(turn_y)
    dy_out[...] = cos_turns(turn_y + 0.25) * rate_y

    step = wave_ref.shape[1]
    order = iota((40, step), 0)
    along_x, along_y, along_z = wave_ref[0:1, :], wave_ref[1:2, :], wave_ref[2:3, :]
    matches_z = ((order & 3) + 1 == along_z) & (order < HX * LZ)
    plus = matches_z & ((order >> 2) == along_x)
    minus = matches_z & ((order >> 2) == -along_x) & (order >= LZ)
    lanes = iota((NY, step), 0)
    up = (lanes == along_y).astype(F32).astype(BF16)
    down = (-lanes - 1 == along_y).astype(F32).astype(BF16)
    both = jnp.concatenate([up] * 4 + [down] * 4, axis=0)
    plus = mm(plus.astype(F32).astype(BF16), both, NT)
    minus = mm(minus.astype(F32).astype(BF16), both, NT)
    order = iota((40, 128), 0)
    lanes = iota((40, 128), 1)
    wave_b = (lanes & (NY - 1)).astype(F32)
    kx = (order >> 2).astype(F32) * (TWO_PI / extent_x)
    kz = ((order & 3) + 1).astype(F32) * (TWO_PI / BOX_HEIGHT)

    def weights(ky):
        squared = kx * kx + ky * ky + kz * kz
        return jnp.exp(-squared / (4.0 * SPLITTING**2)) / squared / atoms_all

    green_up = weights(wave_b * (TWO_PI / extent_y))
    green_down = weights((wave_b + 1.0) * (TWO_PI / extent_y))
    pp, pm = green_up * plus[:, 0:128], green_down * plus[:, 128:256]
    mp, mn = green_up * minus[:, 0:128], green_down * minus[:, 128:256]
    quarter = lanes >> 5
    sign_t = jnp.where((quarter == 1) | (quarter == 2), 1.0, -1.0)
    sign_st = jnp.where((quarter & 1) == 1, 1.0, -1.0)
    sign_s = jnp.where(quarter >= 2, 1.0, -1.0)
    table_out[0] = (pp + pm) + (mp + mn)
    table_out[1] = sign_t * ((pp - pm) + (mp - mn))
    table_out[2] = sign_st * ((pp - pm) - (mp - mn))
    table_out[3] = sign_s * ((pp + pm) - (mp + mn))

    col = iota((NB, 64), 1)
    sub = iota((NB, 64), 0)
    pick_b = ((col >> 3) == sub).astype(F32)
    pick_s = ((col & 7) == sub).astype(F32)
    message = message_ref[...]
    channels = message.shape[0]
    radial = radial_ref[...].T
    spread = mm(message, pick_s, NN, HIGHEST)
    for which in range(2):
        narrow = mm(radial[which * channels : (which + 1) * channels], pick_b, NN, HIGHEST) * spread
        narrow_out[which] = narrow.T
    charge_out[...] = charge_ref[...].T


def basis_terms(dist, rho, live):
    envelope = jnp.exp(-0.25 * rho) * live
    out = []
    for b in range(NB):
        off = dist - CENTRE_STEP * b
        out.append((jnp.exp(off * off * (-0.5 / CENTRE_STEP**2)) * envelope, off))
    return out


def forward_kernel(
    where_ref,
    pos_ref,
    species_ref,
    mid_ref,
    first_ref,
    second_ref,
    nbr_ref,
    embed_ref,
    wide_ref,
    scalar_ref,
    vector_ref,
    hidden_ref,
    readout_ref,
    weight_ref,
    x_ref,
    zy_ref,
    unit_ref,
    energy_out,
    charge_out,
    hbar_out,
    slope_out,
    vsum_out,
    geo_out,
    keep_out,
    send_out,
    tab_ref,
    moment_ref,
    qh_ref,
    ql_ref,
    pay_ref,
    halo_ref,
    sems,
):
    atoms = pos_ref.shape[1]
    tiles = atoms // 128
    copies = [
        pltpu.make_async_copy(ref, halo_ref.at[n], sems.at[n]) for n, ref in enumerate((mid_ref, first_ref, second_ref))
    ]
    for copy in copies:
        copy.start()
    for c in range(3):
        for j in range(tiles):
            tab_ref[c, j : j + 1, :] = pos_ref[c : c + 1, pl.ds(128 * j, 128)]
    for j in range(tiles):
        tab_ref[3, j : j + 1, :] = species_ref[:, pl.ds(128 * j, 128)].astype(F32)
    for copy in copies:
        copy.wait()
    even = (where_ref[1] & 1) == 0
    for i in range(3):
        first, second = halo_ref[1, i], halo_ref[2, i]
        prev, after = jnp.where(even, second, first), jnp.where(even, first, second)
        for j, block in enumerate((prev, halo_ref[0, i], after)):
            shifts = (i - 1.0, j - 1.0, 0.0, 0.0)
            for c in range(4):
                for h in range(2):
                    at = tiles + 2 * (3 * i + j) + h
                    tab_ref[c, at : at + 1, :] = block[c : c + 1, 128 * h : 128 * h + 128] + shifts[c]

    def lane_tile(t, carry):
        lanes = pl.ds(pl.multiple_of(t * 128, 128), 128)
        for tile in range(4):
            index = nbr_ref[pl.ds(8 * tile, 8), lanes]
            live = (index >= 0).astype(F32)
            index = jnp.maximum(index, 0)
            high, low = index >> 7, index & 127
            value = [jnp.zeros((8, 128), F32) for _ in range(4)]
            for block in range(tiles + 18):
                if block // 2 == tiles // 2 + 4:
                    continue
                here = high == block
                for c in range(4):
                    source = jnp.broadcast_to(tab_ref[c, block : block + 1, :], (8, 128))
                    value[c] = jnp.where(here, jnp.take_along_axis(source, low, axis=1), value[c])
            rx, ry, rz = (value[c] - pos_ref[c : c + 1, lanes] for c in range(3))
            rho = rx * rx + ry * ry + rz * rz
            dist = jnp.sqrt(rho + SOFTENING)
            inv = 1.0 / dist
            rows = pl.ds(8 * tile, 8)
            geo_out[0, rows, lanes] = rx * inv
            geo_out[1, rows, lanes] = ry * inv
            geo_out[2, rows, lanes] = rz * inv
            geo_out[3, rows, lanes] = dist
            geo_out[4, rows, lanes] = rho
            geo_out[5, rows, lanes] = value[3]
            geo_out[6, rows, lanes] = live
        dist = geo_out[3, :, lanes]
        terms = basis_terms(dist, geo_out[4, :, lanes], geo_out[6, :, lanes])
        kind = geo_out[5, :, lanes]
        for f in range(4):
            for b in range(NB):
                value = terms[b][0] if f == 0 else terms[b][0] * geo_out[f - 1, :, lanes]
                for s in range(NS):
                    chosen = jnp.where(kind == float(s), value, 0.0)
                    total = (chosen[0:8] + chosen[8:16]) + (chosen[16:24] + chosen[24:32])
                    moment_ref[f, pl.ds(8 * (8 * b + s), 8), lanes] = total
        return carry

    lax.fori_loop(0, tiles, lane_tile, 0, unroll=2)

    def gathered(f):
        wide = wide_ref[0 if f == 0 else 1]
        high, low = parts(moment_ref[f])
        both = mm(wide, high)
        return both[0:128] + both[128:256] + mm(wide[0:128], low)

    scalar_sum = gathered(0)
    norm = None
    for c in range(3):
        vector = gathered(c + 1)
        vsum_out[c] = vector
        norm = vector * vector if norm is None else norm + vector * vector
    update = mm3(scalar_ref[...].T, scalar_sum) + mm3(vector_ref[...].T, norm)
    feature = jnp.zeros_like(update)
    kinds = species_ref[...]
    for s in range(NS):
        feature = jnp.where(kinds == s, embed_ref[:, s : s + 1], feature)
    act, slope = silu_parts(update)
    slope_out[...] = slope
    hidden = feature + act
    act, slope = silu_parts(mm3(hidden_ref[...].T, hidden))
    readout = jnp.broadcast_to(readout_ref[...], (8, 128)).T[:, 0:1]
    energy_out[...] = jnp.sum(act * readout, axis=0, keepdims=True)
    hbar_out[...] = mm3(hidden_ref[...], slope * readout)
    charges = mm3(weight_ref[...], hidden)
    charge_out[...] = charges

    total = jnp.sum(charges, axis=1, keepdims=True)
    local = total * (1.0 / atoms)
    centred = charges - local
    for k in range(XF):
        high, low = parts(centred * x_ref[k : k + 1, :])
        qh_ref[32 * k : 32 * k + 32, :] = high
        ql_ref[32 * k : 32 * k + 32, :] = low
    high, low = qh_ref[...], ql_ref[...]
    for l in range(LZ):
        near, rest = (zy_ref[part, 128 * l : 128 * l + 128, :] for part in range(2))
        slab = mm(high, near, NT) + (mm(low, near, NT) + mm(high, rest, NT))
        unit = unit_ref[l]
        for k in range(XF):
            at = SLAB * l + 32 * k
            pay_ref[at : at + 32, :] = slab[32 * k : 32 * k + 32] + local * unit[k : k + 1]
        pay_ref[UNIT_ROW + XROWS * l : UNIT_ROW + XROWS * (l + 1), :] = unit
    pay_ref[TOTAL_ROW : TOTAL_ROW + 32, :] = jnp.broadcast_to(total, (32, 128))
    half = ROWS // 2
    core = where_ref[0] & 1
    keep_out[...] = pay_ref[pl.ds(pl.multiple_of(core * half, 8), half), :]
    send_out[...] = pay_ref[pl.ds(pl.multiple_of((1 - core) * half, 8), half), :]


def quarters(x, which):
    lane = iota(x.shape, 1)
    if which == 2:
        return pltpu.roll(x, 64, 1)
    even = ((lane >> 5) & 1) == 0
    if which == 1:
        return jnp.where(even, pltpu.roll(x, 96, 1), pltpu.roll(x, 32, 1))
    return jnp.where(even, pltpu.roll(x, 32, 1), pltpu.roll(x, 96, 1))


def backward_kernel(
    atoms_all,
    where_ref,
    near_ref,
    far_ref,
    table_ref,
    x_ref,
    zy_ref,
    energy_ref,
    charge_ref,
    hbar_ref,
    slope_ref,
    vsum_ref,
    geo_ref,
    nbr_ref,
    scalar_ref,
    vector_ref,
    weight_ref,
    narrow_ref,
    site_out,
    neutral_out,
    vh_out,
    vl_out,
    own_out,
    mid_out,
    first_out,
    second_out,
    sum_ref,
    g_ref,
    rbar_ref,
):
    atoms = nbr_ref.shape[1]
    tiles = atoms // 128
    half = ROWS // 2
    core = where_ref[0] & 1
    sum_ref[pl.ds(pl.multiple_of(core * half, 8), half), :] = near_ref[...]
    sum_ref[pl.ds(pl.multiple_of((1 - core) * half, 8), half), :] = far_ref[...]
    mean = sum_ref[TOTAL_ROW : TOTAL_ROW + 32, :] * (1.0 / atoms_all)

    def put(l, k, value):
        rows = pl.ds(pl.multiple_of(k * 32, 32), 32)
        high, low = parts(value)
        vh_out[rows, 128 * l : 128 * l + 128] = high
        vl_out[rows, 128 * l : 128 * l + 128] = low

    def tile_of(l, k):
        unit = sum_ref[pl.ds(UNIT_ROW + XROWS * l + k, 1), :]
        rows = pl.ds(pl.multiple_of(SLAB * l + k * 32, 32), 32)
        return sum_ref[rows, :] - mean * unit, unit

    overlap = jnp.zeros((32, 128), F32)
    for l in range(LZ):
        cos_tile, unit = tile_of(l, 0)
        g0 = table_ref[0, l : l + 1, :]
        gt = table_ref[1, l : l + 1, :]
        value = g0 * cos_tile + gt * quarters(cos_tile, 3)
        overlap = overlap + value * unit
        put(l, 0, value)

    def mix(a, overlap):
        for l in range(LZ):
            cos_tile, cos_unit = tile_of(l, a)
            sin_tile, sin_unit = tile_of(l, a + HX - 1)
            g0, gt, gst, gs = (table_ref[n, pl.ds(a * LZ + l, 1), :] for n in range(4))
            value = (g0 * cos_tile + gt * quarters(cos_tile, 3)) + (
                gst * quarters(sin_tile, 1) + gs * quarters(sin_tile, 2)
            )
            overlap = overlap + value * cos_unit
            put(l, a, value)
            value = (g0 * sin_tile + gt * quarters(sin_tile, 3)) - (
                gst * quarters(cos_tile, 1) + gs * quarters(cos_tile, 2)
            )
            overlap = overlap + value * sin_unit
            put(l, a + HX - 1, value)
        return overlap

    overlap = lax.fori_loop(1, HX, mix, overlap, unroll=4)
    potential_mean = jnp.sum(overlap, axis=1, keepdims=True) * (1.0 / atoms_all)

    spread = mm(vh_out[...], zy_ref[0]) + (mm(vl_out[...], zy_ref[0]) + mm(vh_out[...], zy_ref[1]))
    potential = jnp.zeros((32, atoms), F32)
    for k in range(XF):
        potential = potential + x_ref[k : k + 1, :] * spread[32 * k : 32 * k + 32]
    neutral = charge_ref[...] - mean[:, 0:1]
    neutral_out[...] = neutral
    site_out[...] = energy_ref[...] + jnp.sum(neutral * potential, axis=0, keepdims=True)
    charge_bar = 2.0 * (potential - potential_mean)
    update_bar = (hbar_ref[...] + mm3(weight_ref[...], charge_bar)) * slope_ref[...]
    scalar_bar = mm3(scalar_ref[...], update_bar)
    norm_bar = 2.0 * mm3(vector_ref[...], update_bar)
    g_ref[0] = mm3(narrow_ref[0], scalar_bar)
    for c in range(3):
        g_ref[c + 1] = mm3(narrow_ref[1], vsum_ref[c] * norm_bar)

    def slots(t, carry):
        lanes = pl.ds(pl.multiple_of(t * 128, 128), 128)
        own = [jnp.zeros((8, 128), F32) for _ in range(3)]
        for tile in range(4):
            rows = pl.ds(8 * tile, 8)
            unit = [geo_ref[c, rows, lanes] for c in range(3)]
            dist = geo_ref[3, rows, lanes]
            kind = geo_ref[5, rows, lanes].astype(jnp.int32)
            terms = basis_terms(dist, geo_ref[4, rows, lanes], geo_ref[6, rows, lanes])
            inv = 1.0 / dist
            ubar = [jnp.zeros((8, 128), F32) for _ in range(3)]
            plain = jnp.zeros((8, 128), F32)
            tilted = jnp.zeros((8, 128), F32)
            for b in range(NB):
                value, off = terms[b]
                picked = [
                    jnp.take_along_axis(g_ref[f, 8 * b : 8 * b + 8, lanes], kind, axis=0) for f in range(4)
                ]
                bar = picked[0]
                for c in range(3):
                    bar = bar + unit[c] * picked[c + 1]
                    ubar[c] = ubar[c] + value * picked[c + 1]
                bar = bar * value
                plain = plain + bar
                tilted = tilted + bar * off
            along = ubar[0] * unit[0] + ubar[1] * unit[1] + ubar[2] * unit[2]
            dist_bar = tilted * (-1.0 / CENTRE_STEP**2) - along * inv
            radial = dist * (2.0 * (-0.25 * plain) + dist_bar * inv)
            for c in range(3):
                bar = ubar[c] * inv + unit[c] * radial
                rbar_ref[c, rows, lanes] = bar
                own[c] = own[c] + bar
        for c in range(3):
            own_out[c : c + 1, lanes] = -jnp.sum(own[c], axis=0, keepdims=True)
        return carry

    lax.fori_loop(0, tiles, slots, 0)

    block_rows = 24
    rows_high = iota((block_rows, atoms), 0)
    rows_low = iota((128, atoms), 0)

    def scatter(s, total):
        index = jnp.maximum(nbr_ref[pl.ds(s, 1), :], 0)
        at_high = rows_high == (index >> 7)
        at_low = jnp.where(rows_low == (index & 127), 1.0, 0.0).astype(BF16)
        pieces = []
        for c in range(3):
            value = rbar_ref[c, pl.ds(s, 1), :]
            high = value.astype(BF16).astype(F32)
            pieces.append(jnp.where(at_high, high, 0.0))
            pieces.append(jnp.where(at_high, value - high, 0.0))
        left = jnp.concatenate(pieces, axis=0).astype(BF16)
        return total + mm(left, at_low, NT)

    even = (where_ref[1] & 1) == 0
    total = lax.fori_loop(0, nbr_ref.shape[0], scatter, jnp.zeros((6 * block_rows, 128), F32), unroll=16)
    for c in range(3):
        at = 2 * block_rows * c
        table = total[at : at + block_rows] + total[at + block_rows : at + 2 * block_rows]
        for j in range(tiles):
            lanes = pl.ds(128 * j, 128)
            own_out[c : c + 1, lanes] = own_out[c : c + 1, lanes] + table[j : j + 1]
        for i in range(3):
            for h in range(2):
                lanes = slice(128 * h, 128 * h + 128)
                prev, mid, after = (table[row : row + 1] for row in (tiles + 2 * (3 * i + j) + h for j in range(3)))
                mid_out[i, c : c + 1, lanes] = mid
                first_out[i, c : c + 1, lanes] = jnp.where(even, after, prev)
                second_out[i, c : c + 1, lanes] = jnp.where(even, prev, after)


def ewald_kernel(
    extent_y,
    vh_ref,
    vl_ref,
    x_ref,
    dx_ref,
    z_ref,
    dz_ref,
    y_ref,
    dy_ref,
    zy_ref,
    neutral_ref,
    own_ref,
    out_ref,
    high_ref,
    low_ref,
):
    neutral = neutral_ref[...]
    coefficient_high, coefficient_low = vh_ref[...], vl_ref[...]

    def total(c, functions, high, low):
        spread = mm(coefficient_high, high) + (mm(coefficient_low, high) + mm(coefficient_high, low))
        field = None
        for k in range(XF):
            term = functions[k : k + 1, :] * spread[32 * k : 32 * k + 32]
            field = term if field is None else field + term
        out_ref[c : c + 1, :] = own_ref[c : c + 1, :] + 2.0 * jnp.sum(neutral * field, axis=0, keepdims=True)

    total(0, dx_ref, zy_ref[0], zy_ref[1])
    for c in (2, 1):
        for l in range(LZ):
            for half in range(2):
                at = 2 * l + half
                turned = dz_ref[at : at + 1, :]
                if c == 2:
                    value = (TWO_PI / BOX_HEIGHT * (l + 1)) * turned * y_ref[...]
                else:
                    value = z_ref[at : at + 1, :] * dy_ref[...] - (0.5 * TWO_PI / extent_y) * turned * y_ref[...]
                high, low = parts(value)
                high_ref[64 * at : 64 * at + 64, :] = high
                low_ref[64 * at : 64 * at + 64, :] = low
        total(c, x_ref, high_ref[...], low_ref[...])


def finish_kernel(base_ref, mid_ref, first_ref, second_ref, ghost_ref, out_ref, back_ref, sems):
    atoms = base_ref.shape[1]
    copies = [
        pltpu.make_async_copy(ref, back_ref.at[n], sems.at[n]) for n, ref in enumerate((mid_ref, first_ref, second_ref))
    ]
    for copy in copies:
        copy.start()
    for copy in copies:
        copy.wait()
    returned = back_ref[0] + back_ref[1] + back_ref[2]
    high = returned.astype(BF16).astype(F32)
    rest = returned - high
    middle = rest.astype(BF16).astype(F32)
    split = jnp.concatenate([high, middle, rest - middle, jnp.zeros((7, 256), F32)], axis=0).astype(BF16)
    at = jnp.where(iota((atoms, 256), 0) == ghost_ref[...], 1.0, 0.0).astype(BF16)
    spread = mm(split, at, NT)
    out_ref[...] = -(base_ref[...] + ((spread[0:3] + spread[3:6]) + spread[6:9]))


def swapped(array, axis, far):
    n = lax.axis_size(axis)
    pairs = [(i, (i + (1 if i % 2 else -1)) % n if far else i ^ 1) for i in range(n)]
    return lax.ppermute(array, axis, pairs)


def along_z(array, flip):
    first, second = lax.axis_size("gx"), lax.axis_size("gy")
    pairs = []
    for device in range(first * second):
        u, v = divmod(device, second)
        z = (v // 16 * 4 + u // 2) ^ flip
        pairs.append((device, (z % 4 * 2 + u % 2) * second + z // 4 * 16 + v % 16))
    return lax.ppermute(array, AXES, pairs)


def across_plane(array):
    planes = [list(range(16 * k, 16 * k + 16)) for k in range(lax.axis_size("gy") // 16)]
    return lax.all_to_all(array, "gy", 0, 0, tiled=True, axis_index_groups=planes)


def reduced(keep, send):
    keep = keep + swapped(send, "gx", False)
    got = across_plane(keep.reshape(16, -1, 128))
    return sum((got[k] for k in range(1, 16)), got[0])


def spread_out(keep):
    for flip in (1, 2, 7):
        keep = keep + along_z(keep, flip)
    keep = across_plane(jnp.broadcast_to(keep, (16,) + keep.shape)).reshape(-1, 128)
    return keep, swapped(keep, "gx", False)


def shards(
    positions,
    species,
    neighbours,
    ghost_index,
    wave_index,
    embedding,
    radial_weight,
    message_weight,
    scalar_weight,
    vector_weight,
    readout_hidden,
    readout_vector,
    charge_weight,
):
    atoms = positions.shape[1]
    extents = lax.axis_size("gx"), lax.axis_size("gy")
    atoms_all = atoms * extents[0] * extents[1]
    where = jnp.stack([lax.axis_index("gx"), lax.axis_index("gy")])
    kinds = species[None]
    ghosts = ghost_index[None]

    (border,) = call(border_kernel, [((4, 256), F32)], [pltpu.VMEM((8, atoms), F32)], spaces="vvv", vmem=4)(positions, kinds, ghosts)
    even = (where[0] & 1) == 0
    second, first = swapped(border, "gx", True), swapped(border, "gx", False)
    mid = jnp.stack([jnp.where(even, second, first), border, jnp.where(even, first, second)])
    second, first = swapped(mid, "gy", True), swapped(mid, "gy", False)

    fx, zy, unit, wide, embed, message = call(
        functools.partial(prepare_kernel, extents),
        [
            ((XROWS, atoms), F32),
            ((2, 128 * LZ, atoms), BF16),
            ((LZ, XROWS, 128), F32),
            ((2, 256, 512), BF16),
            ((128, 8), F32),
            ((128, 8), F32),
        ],
        spaces="svvvv",
        vmem=16,
        flops=10**9,
        nbytes=2 * 10**6,
    )(where, positions, embedding, radial_weight, message_weight)

    nbr = neighbours.T
    charge_t = charge_weight.T
    energy, charge, hbar, slope, vsum, geo, keep, send = call(
        forward_kernel,
        [
            ((1, atoms), F32),
            ((32, atoms), F32),
            ((128, atoms), F32),
            ((128, atoms), F32),
            ((3, 128, atoms), F32),
            ((7, 32, atoms), F32),
            ((ROWS // 2, 128), F32),
            ((ROWS // 2, 128), F32),
        ],
        [
            pltpu.VMEM((4, 24, 128), F32),
            pltpu.VMEM((4, 512, atoms), F32),
            pltpu.VMEM((SLAB, atoms), BF16),
            pltpu.VMEM((SLAB, atoms), BF16),
            pltpu.VMEM((ROWS, 128), F32),
            pltpu.VMEM((3, 3, 4, 256), F32),
            pltpu.SemaphoreType.DMA((3,)),
        ],
        spaces="svvaaa" + "v" * 11,
        vmem=28,
        flops=5 * 10**9,
        nbytes=4 * 10**6,
    )(
        where,
        positions,
        kinds,
        mid,
        first,
        second,
        nbr,
        embed,
        wide,
        scalar_weight,
        vector_weight,
        readout_hidden,
        readout_vector[None],
        charge_t,
        fx,
        zy,
        unit,
    )

    keep = reduced(keep, send)
    keep, waves_late, message = lax.optimization_barrier((keep, wave_index, message))
    table, narrow, weight, dx, fz, dz, fy, dy = call(
        functools.partial(later_kernel, extents, atoms_all),
        [
            ((4, 40, 128), F32),
            ((2, 64, 128), F32),
            ((128, 32), F32),
            ((XROWS, atoms), F32),
            ((2 * LZ, atoms), F32),
            ((2 * LZ, atoms), F32),
            ((2 * NY, atoms), F32),
            ((2 * NY, atoms), F32),
        ],
        spaces="svvvvv",
        vmem=16,
        flops=10**9,
        nbytes=2 * 10**6,
    )(where, positions, waves_late, radial_weight, message, charge_t)
    near, far = spread_out(keep)

    site, neutral, vh, vl, own, g_mid, g_first, g_second = call(
        functools.partial(backward_kernel, atoms_all),
        [
            ((1, atoms), F32),
            ((32, atoms), F32),
            ((SLAB, 128 * LZ), BF16),
            ((SLAB, 128 * LZ), BF16),
            ((3, atoms), F32),
            ((3, 3, 256), F32),
            ((3, 3, 256), F32),
            ((3, 3, 256), F32),
        ],
        [
            pltpu.VMEM((ROWS, 128), F32),
            pltpu.VMEM((4, 64, atoms), F32),
            pltpu.VMEM((3, 32, atoms), F32),
        ],
        spaces="s" + "v" * 16,
        vmem=28,
        flops=5 * 10**9,
        nbytes=4 * 10**6,
    )(
        where,
        near,
        far,
        table,
        fx,
        zy,
        energy,
        charge,
        hbar,
        slope,
        vsum,
        geo,
        nbr,
        scalar_weight,
        vector_weight,
        weight,
        narrow,
    )

    second, first = swapped(g_second, "gy", True), swapped(g_first, "gy", False)
    (base,) = call(
        functools.partial(ewald_kernel, extents[1]),
        [((3, atoms), F32)],
        [pltpu.VMEM((128 * LZ, atoms), BF16)] * 2,
        spaces="v" * 11,
        vmem=24,
        flops=5 * 10**9,
        nbytes=4 * 10**6,
    )(vh, vl, fx, dx, fz, dz, fy, dy, zy, neutral, own)
    first, second, base = lax.optimization_barrier((first, second, base))
    column = g_mid + first + second
    second = swapped(jnp.where(even, column[0], column[2]), "gx", True)
    first = swapped(jnp.where(even, column[2], column[0]), "gx", False)
    (forces,) = call(
        finish_kernel,
        [((3, atoms), F32)],
        [pltpu.VMEM((3, 3, 256), F32), pltpu.SemaphoreType.DMA((3,))],
        spaces="vaaav",
        vmem=4,
    )(base, column[1], first, second, ghosts)
    return forces, site[0]


def solution(mesh):
    return jax.shard_map(
        shards,
        mesh=mesh,
        in_specs=(
            P(None, ("gx", "gy")),
            P(("gx", "gy")),
            P(("gx", "gy"), None),
            P(("gx", "gy")),
            P(),
            P(),
            P(),
            P(),
            P(),
            P(),
            P(),
            P(),
            P(),
        ),
        out_specs=(P(None, ("gx", "gy")), P(("gx", "gy"))),
        check_vma=False,
    )
```

```python
import functools

import jax
import jax.numpy as jnp
from jax import lax
from jax.experimental import pallas as pl
from jax.experimental.pallas import tpu as pltpu
from jax.sharding import PartitionSpec as P

NB = 8
NS = 8
HIGHEST = lax.Precision.HIGHEST
TWO_PI = 6.283185307179586
BOX_HEIGHT = 4.0
SPLITTING = 2.5
SOFTENING = 0.01
CENTRE_STEP = 0.3
AXES = ("gx", "gy")

HX = 9
LZ = 4
NY = 32
XF = 2 * HX - 1
XROWS = 24
SLAB = XF * 32
UNIT_ROW = 2 * SLAB
TOTAL_ROW = UNIT_ROW + 2 * XROWS
HALF = TOTAL_ROW + 16

F32 = jnp.float32
BF16 = jnp.bfloat16
NT = (((1,), (1,)), ((), ()))
NN = (((1,), (0,)), ((), ()))


def mm(a, b, dims=NN, precision=None):
    return lax.dot_general(a, b, dims, precision=precision, preferred_element_type=F32)


def parts(x):
    high = x.astype(BF16)
    return high, (x - high.astype(F32)).astype(BF16)


def mm3(a, b, dims=NN):
    a_high, a_low = parts(a)
    b_high, b_low = parts(b)
    return mm(a_high, b_high, dims) + (mm(a_low, b_high, dims) + mm(a_high, b_low, dims))


def cos_turns(t):
    r = t - jnp.floor(t + 0.5)
    s = (0.25 - jnp.abs(r)) * TWO_PI
    q = s * s
    p = -2.5052108e-08 + q * 1.6059044e-10
    p = 2.7557319e-06 + q * p
    p = -1.9841270e-04 + q * p
    p = 8.3333333e-03 + q * p
    p = -1.6666667e-01 + q * p
    return s + s * (q * p)


def silu_parts(x):
    gate = 1.0 / (1.0 + jnp.exp(-x))
    return x * gate, gate * (1.0 + x * (1.0 - gate))


def iota(shape, dim):
    return lax.broadcasted_iota(jnp.int32, shape, dim)


def call(kernel, outs, scratch=(), spaces="", flops=0, nbytes=0, vmem=56):
    known = {"s": pltpu.SMEM, "v": pltpu.VMEM, "a": pl.ANY, "h": pltpu.HBM}
    return pl.pallas_call(
        kernel,
        in_specs=[pl.BlockSpec(memory_space=known[letter]) for letter in spaces],
        out_shape=[jax.ShapeDtypeStruct(s, d) for s, d in outs],
        scratch_shapes=list(scratch),
        compiler_params=pltpu.CompilerParams(vmem_limit_bytes=vmem * 2**20),
        cost_estimate=pl.CostEstimate(flops=flops, bytes_accessed=nbytes, transcendentals=0),
    )


def border_kernel(pos_ref, species_ref, ghost_ref, out_ref, tab_ref):
    atoms = pos_ref.shape[1]
    tab_ref[0:3, :] = pos_ref[...]
    tab_ref[3:4, :] = species_ref[...].astype(F32)
    for part in range(ghost_ref.shape[1] // 128):
        lanes = pl.ds(128 * part, 128)
        index = jnp.broadcast_to(ghost_ref[:, lanes], (8, 128))
        high, low = index >> 7, index & 127
        value = jnp.zeros((8, 128), F32)
        for block in range(atoms // 128):
            source = tab_ref[:, pl.ds(128 * block, 128)]
            value = jnp.where(high == block, jnp.take_along_axis(source, low, axis=1), value)
        out_ref[:, lanes] = value[0:4]


def waves(grid, where_ref, pos_ref):
    extent_x, extent_y = grid
    atoms = pos_ref.shape[1]
    u, v = where_ref[0], where_ref[1]
    x, y, z = pos_ref[0:1, :], pos_ref[1:2, :], pos_ref[2:3, :]

    row = iota((XROWS, atoms), 0)
    order = jnp.where(row < HX, row, row - (HX - 1))
    whole = lax.rem(order * u, extent_x).astype(F32)
    order = order.astype(F32)
    turn_x = (order * x + whole) / extent_x - jnp.where(row < HX, 0.0, 0.25)
    rate_x = jnp.where(row < XF, order * (TWO_PI / extent_x), 0.0)

    row = iota((2 * LZ, atoms), 0)
    whole = lax.rem(v, 2 * extent_y).astype(F32)
    turn_z = ((row >> 1) + 1).astype(F32) * z * (1.0 / BOX_HEIGHT) - (y + whole) * (0.5 / extent_y)
    turn_z = turn_z - 0.25 * (row & 1).astype(F32)

    row = iota((2 * NY, atoms), 0)
    twice = 2 * (row & (NY - 1)) + 1
    whole = lax.rem(twice * v, 2 * extent_y).astype(F32)
    twice = twice.astype(F32)
    turn_y = (twice * y + whole) * (0.5 / extent_y) - jnp.where(row < NY, 0.0, 0.25)
    return turn_x, rate_x, turn_z, turn_y, twice * (0.5 * TWO_PI / extent_y)


def prepare_kernel(
    grid,
    where_ref,
    pos_ref,
    embed_ref,
    radial_ref,
    message_ref,
    readout_ref,
    x_out,
    zy_out,
    unit_out,
    weight_out,
    weight_t_out,
    embed_out,
    readout_out,
):
    turn_x, _, turn_z, turn_y, _ = waves(grid, where_ref, pos_ref)
    fx = jnp.where(iota(turn_x.shape, 0) < XF, cos_turns(turn_x), 0.0)
    fz, fy = cos_turns(turn_z), cos_turns(turn_y)
    x_out[...] = fx

    for l in range(LZ):
        zy = jnp.concatenate([fz[2 * l : 2 * l + 1] * fy, fz[2 * l + 1 : 2 * l + 2] * fy], axis=0)
        high, low = parts(zy)
        zy_out[0, 128 * l : 128 * l + 128] = high
        zy_out[1, 128 * l : 128 * l + 128] = low
        unit_out[l] = mm(fx, zy, NT, HIGHEST)

    embed = embed_ref[...].T
    message = mm(message_ref[...].T, embed, NN, HIGHEST)
    embed_out[...] = embed
    readout_out[...] = jnp.broadcast_to(readout_ref[...], (8, 128)).T
    col = iota((NB, 64), 1)
    sub = iota((NB, 64), 0)
    pick_b = ((col >> 3) == sub).astype(F32)
    pick_s = ((col & 7) == sub).astype(F32)
    spread = mm(message, pick_s, NN, HIGHEST)
    radial = radial_ref[...].T
    channels = message.shape[0]
    for which in range(2):
        weight = mm(radial[which * channels : (which + 1) * channels], pick_b, NN, HIGHEST) * spread
        weight_out[which] = weight
        weight_t_out[which] = weight.T


def later_kernel(
    grid,
    atoms_all,
    wave_ref,
    charge_ref,
    table_out,
    charge_out,
):
    extent_x, extent_y = grid

    step = wave_ref.shape[1]
    order = iota((40, step), 0)
    along_x, along_y, along_z = wave_ref[0:1, :], wave_ref[1:2, :], wave_ref[2:3, :]
    matches_z = ((order & 3) + 1 == along_z) & (order < HX * LZ)
    plus = matches_z & ((order >> 2) == along_x)
    minus = matches_z & ((order >> 2) == -along_x) & (order >= LZ)
    lanes = iota((NY, step), 0)
    up = (lanes == along_y).astype(F32).astype(BF16)
    down = (-lanes - 1 == along_y).astype(F32).astype(BF16)
    both = jnp.concatenate([up] * 4 + [down] * 4, axis=0)
    plus = mm(plus.astype(F32).astype(BF16), both, NT)
    minus = mm(minus.astype(F32).astype(BF16), both, NT)
    order = iota((40, 128), 0)
    lanes = iota((40, 128), 1)
    wave_b = (lanes & (NY - 1)).astype(F32)
    kx = (order >> 2).astype(F32) * (TWO_PI / extent_x)
    kz = ((order & 3) + 1).astype(F32) * (TWO_PI / BOX_HEIGHT)

    def weights(ky):
        squared = kx * kx + ky * ky + kz * kz
        return jnp.exp(-squared / (4.0 * SPLITTING**2)) / squared / atoms_all

    green_up = weights(wave_b * (TWO_PI / extent_y))
    green_down = weights((wave_b + 1.0) * (TWO_PI / extent_y))
    pp, pm = green_up * plus[:, 0:128], green_down * plus[:, 128:256]
    mp, mn = green_up * minus[:, 0:128], green_down * minus[:, 128:256]
    quarter = lanes >> 5
    sign_t = jnp.where((quarter == 1) | (quarter == 2), 1.0, -1.0)
    sign_st = jnp.where((quarter & 1) == 1, 1.0, -1.0)
    sign_s = jnp.where(quarter >= 2, 1.0, -1.0)
    table_out[0] = (pp + pm) + (mp + mn)
    table_out[1] = sign_t * ((pp - pm) + (mp - mn))
    table_out[2] = sign_st * ((pp - pm) - (mp - mn))
    table_out[3] = sign_s * ((pp + pm) - (mp + mn))

    charge_out[...] = charge_ref[...].T


def basis_terms(dist, rho, live):
    envelope = jnp.exp(-0.25 * rho) * live
    out = []
    for b in range(NB):
        off = dist - CENTRE_STEP * b
        out.append((jnp.exp(off * off * (-0.5 / CENTRE_STEP**2)) * envelope, off))
    return out


def forward_kernel(
    where_ref,
    pos_ref,
    species_ref,
    mid_ref,
    first_ref,
    second_ref,
    nbr_ref,
    embed_ref,
    pair_ref,
    scalar_ref,
    vector_ref,
    hidden_ref,
    readout_ref,
    weight_ref,
    x_ref,
    zy_ref,
    unit_ref,
    charge_out,
    hbar_out,
    slope_out,
    vsum_out,
    geo_out,
    keep_out,
    send_out,
    tab_ref,
    moment_ref,
    qh_ref,
    ql_ref,
    halo_ref,
    sems,
):
    atoms = pos_ref.shape[1]
    tiles = atoms // 128
    copies = [
        pltpu.make_async_copy(ref, halo_ref.at[n], sems.at[n]) for n, ref in enumerate((mid_ref, first_ref, second_ref))
    ]
    for copy in copies:
        copy.start()
    for c in range(3):
        for j in range(tiles):
            tab_ref[c, j : j + 1, :] = pos_ref[c : c + 1, pl.ds(128 * j, 128)]
    for j in range(tiles):
        tab_ref[3, j : j + 1, :] = species_ref[:, pl.ds(128 * j, 128)].astype(F32)
    for copy in copies:
        copy.wait()
    even = (where_ref[0] & 1) == 0
    for j in range(3):
        first, second = halo_ref[1, j], halo_ref[2, j]
        prev, after = jnp.where(even, second, first), jnp.where(even, first, second)
        for i, block in enumerate((prev, halo_ref[0, j], after)):
            shifts = (i - 1.0, j - 1.0, 0.0, 0.0)
            for c in range(4):
                for h in range(2):
                    at = tiles + 2 * (3 * i + j) + h
                    tab_ref[c, at : at + 1, :] = block[c : c + 1, 128 * h : 128 * h + 128] + shifts[c]

    def lane_tile(t, carry):
        lanes = pl.ds(pl.multiple_of(t * 128, 128), 128)
        for tile in range(4):
            index = nbr_ref[pl.ds(8 * tile, 8), lanes]
            live = (index >= 0).astype(F32)
            index = jnp.maximum(index, 0)
            high, low = index >> 7, index & 127
            value = [jnp.zeros((8, 128), F32) for _ in range(4)]
            for block in range(tiles + 18):
                if block // 2 == tiles // 2 + 4:
                    continue
                here = high == block
                for c in range(4):
                    source = jnp.broadcast_to(tab_ref[c, block : block + 1, :], (8, 128))
                    value[c] = jnp.where(here, jnp.take_along_axis(source, low, axis=1), value[c])
            rx, ry, rz = (value[c] - pos_ref[c : c + 1, lanes] for c in range(3))
            rho = rx * rx + ry * ry + rz * rz
            dist = jnp.sqrt(rho + SOFTENING)
            inv = 1.0 / dist
            rows = pl.ds(8 * tile, 8)
            geo_out[0, rows, lanes] = rx * inv
            geo_out[1, rows, lanes] = ry * inv
            geo_out[2, rows, lanes] = rz * inv
            geo_out[3, rows, lanes] = dist
            geo_out[4, rows, lanes] = rho
            geo_out[5, rows, lanes] = value[3]
            geo_out[6, rows, lanes] = live
        dist = geo_out[3, :, lanes]
        terms = basis_terms(dist, geo_out[4, :, lanes], geo_out[6, :, lanes])
        kind = geo_out[5, :, lanes]
        for f in range(4):
            for b in range(NB):
                value = terms[b][0] if f == 0 else terms[b][0] * geo_out[f - 1, :, lanes]
                rows = []
                for s in range(NS):
                    chosen = jnp.where(kind == float(s), value, 0.0)
                    rows.append((chosen[0:8] + chosen[8:16]) + (chosen[16:24] + chosen[24:32]))
                for step in (4, 2, 1):
                    here = (iota((8, 128), 0) & step) == 0
                    rows = [
                        jnp.where(here, one + pltpu.roll(one, 8 - step, 0), two + pltpu.roll(two, step, 0))
                        for one, two in zip(rows[: len(rows) // 2], rows[len(rows) // 2 :])
                    ]
                moment_ref[f, 8 * b : 8 * b + 8, lanes] = rows[0]
        return carry

    lax.fori_loop(0, tiles, lane_tile, 0, unroll=2)

    def gathered(f):
        return mm3(pair_ref[0 if f == 0 else 1], moment_ref[f])

    scalar_sum = gathered(0)
    norm = None
    for c in range(3):
        vector = gathered(c + 1)
        vsum_out[c] = vector
        norm = vector * vector if norm is None else norm + vector * vector
    update = mm3(scalar_ref[...].T, scalar_sum) + mm3(vector_ref[...].T, norm)
    feature = jnp.zeros_like(update)
    kinds = species_ref[...]
    for s in range(NS):
        feature = jnp.where(kinds == s, embed_ref[:, s : s + 1], feature)
    act, slope = silu_parts(update)
    slope_out[...] = slope
    hidden = feature + act
    act, slope = silu_parts(mm3(hidden_ref[...].T, hidden))
    readout = readout_ref[:, 0:1]
    charge_out[32:33, :] = jnp.sum(act * readout, axis=0, keepdims=True)
    hbar_out[...] = mm3(hidden_ref[...], slope * readout)
    charges = mm3(weight_ref[...], hidden)
    charge_out[0:32, :] = charges
    charge_out[33:40, :] = jnp.zeros((7, atoms), F32)

    total = jnp.sum(charges, axis=1, keepdims=True)
    local = total * (1.0 / atoms)
    centred = charges - local
    for k in range(XF):
        high, low = parts(centred * x_ref[k : k + 1, :])
        qh_ref[32 * k : 32 * k + 32, :] = high
        ql_ref[32 * k : 32 * k + 32, :] = low
    high, low = qh_ref[...], ql_ref[...]
    core = where_ref[0] & 1
    for out, half in ((send_out, 1 - core), (keep_out, core)):
        for n in range(2):
            l = 2 * half + n
            near, rest = (zy_ref[part, pl.ds(pl.multiple_of(128 * l, 128), 128), :] for part in range(2))
            slab = mm(high, near, NT) + (mm(low, near, NT) + mm(high, rest, NT))
            unit = unit_ref[l]
            for k in range(XF):
                at = SLAB * n + 32 * k
                out[at : at + 32, :] = slab[32 * k : 32 * k + 32] + local * unit[k : k + 1]
            out[UNIT_ROW + XROWS * n : UNIT_ROW + XROWS * (n + 1), :] = unit
        out[TOTAL_ROW:HALF, :] = jnp.where(iota((16, 128), 1) < 64, total[0:16], total[16:32])


def quarters(x, which):
    lane = iota(x.shape, 1)
    if which == 2:
        return pltpu.roll(x, 64, 1)
    even = ((lane >> 5) & 1) == 0
    if which == 1:
        return jnp.where(even, pltpu.roll(x, 96, 1), pltpu.roll(x, 32, 1))
    return jnp.where(even, pltpu.roll(x, 32, 1), pltpu.roll(x, 96, 1))


def contribution(half, ref, table_ref, x_ref, zy_ref, vh_out, vl_out, atoms_all):
    ends = ref[TOTAL_ROW:HALF, :]
    mean = jnp.concatenate([ends[:, 0:1], ends[:, 64:65]], axis=0) * (1.0 / atoms_all)

    def put(n, k, value):
        rows = pl.ds(pl.multiple_of(k * 32, 32), 32)
        high, low = parts(value)
        vh_out[rows, 128 * n : 128 * n + 128] = high
        vl_out[rows, 128 * n : 128 * n + 128] = low

    def tile_of(n, k):
        unit = ref[pl.ds(UNIT_ROW + XROWS * n + k, 1), :]
        rows = pl.ds(pl.multiple_of(SLAB * n + k * 32, 32), 32)
        return ref[rows, :] - mean * unit, unit

    overlap = jnp.zeros((32, 128), F32)
    for n in range(2):
        cos_tile, unit = tile_of(n, 0)
        g0, gt = (table_ref[t, pl.ds(2 * half + n, 1), :] for t in range(2))
        value = g0 * cos_tile + gt * quarters(cos_tile, 3)
        overlap = overlap + value * unit
        put(n, 0, value)

    def mix(a, overlap):
        for n in range(2):
            cos_tile, cos_unit = tile_of(n, a)
            sin_tile, sin_unit = tile_of(n, a + HX - 1)
            g0, gt, gst, gs = (table_ref[t, pl.ds(a * LZ + 2 * half + n, 1), :] for t in range(4))
            value = (g0 * cos_tile + gt * quarters(cos_tile, 3)) + (
                gst * quarters(sin_tile, 1) + gs * quarters(sin_tile, 2)
            )
            overlap = overlap + value * cos_unit
            put(n, a, value)
            value = (g0 * sin_tile + gt * quarters(sin_tile, 3)) - (
                gst * quarters(cos_tile, 1) + gs * quarters(cos_tile, 2)
            )
            overlap = overlap + value * sin_unit
            put(n, a + HX - 1, value)
        return overlap

    overlap = lax.fori_loop(1, HX, mix, overlap, unroll=8)
    at = pl.ds(pl.multiple_of(256 * half, 256), 256)
    high, low = zy_ref[0, at, :], zy_ref[1, at, :]
    spread = mm(vh_out[...], high) + (mm(vl_out[...], high) + mm(vh_out[...], low))
    potential = jnp.zeros((32, zy_ref.shape[2]), F32)
    for k in range(XF):
        potential = potential + x_ref[k : k + 1, :] * spread[32 * k : 32 * k + 32]
    return mean, potential, overlap


def near_kernel(
    atoms_all, where_ref, near_ref, table_ref, x_ref, zy_ref, vh_out, vl_out, potential_out, overlap_out
):
    half = where_ref[0] & 1
    _, potential, overlap = contribution(half, near_ref, table_ref, x_ref, zy_ref, vh_out, vl_out, atoms_all)
    potential_out[...] = potential
    overlap_out[...] = overlap


def backward_kernel(
    atoms_all,
    where_ref,
    far_ref,
    table_ref,
    x_ref,
    zy_ref,
    potential_ref,
    overlap_ref,
    charge_ref,
    hbar_ref,
    slope_ref,
    vsum_ref,
    geo_ref,
    nbr_ref,
    scalar_ref,
    vector_ref,
    weight_ref,
    pair_ref,
    site_out,
    neutral_out,
    vh_out,
    vl_out,
    own_out,
    mid_out,
    first_out,
    second_out,
    g_ref,
    rbar_ref,
):
    atoms = nbr_ref.shape[1]
    tiles = atoms // 128
    half = 1 - (where_ref[0] & 1)
    mean, potential, overlap = contribution(half, far_ref, table_ref, x_ref, zy_ref, vh_out, vl_out, atoms_all)
    potential = potential + potential_ref[...]
    overlap = overlap + overlap_ref[...]
    potential_mean = jnp.sum(overlap, axis=1, keepdims=True) * (1.0 / atoms_all)
    neutral = charge_ref[0:32, :] - mean
    neutral_out[...] = neutral
    site_out[...] = charge_ref[32:33, :] + jnp.sum(neutral * potential, axis=0, keepdims=True)
    charge_bar = 2.0 * (potential - potential_mean)
    update_bar = (hbar_ref[...] + mm3(weight_ref[...], charge_bar)) * slope_ref[...]
    scalar_bar = mm3(scalar_ref[...], update_bar)
    norm_bar = 2.0 * mm3(vector_ref[...], update_bar)
    g_ref[0] = mm3(pair_ref[0], scalar_bar)
    for c in range(3):
        g_ref[c + 1] = mm3(pair_ref[1], vsum_ref[c] * norm_bar)

    def slots(t, carry):
        lanes = pl.ds(pl.multiple_of(t * 128, 128), 128)
        own = [jnp.zeros((8, 128), F32) for _ in range(3)]
        for tile in range(4):
            rows = pl.ds(8 * tile, 8)
            unit = [geo_ref[c, rows, lanes] for c in range(3)]
            dist = geo_ref[3, rows, lanes]
            kind = geo_ref[5, rows, lanes].astype(jnp.int32)
            terms = basis_terms(dist, geo_ref[4, rows, lanes], geo_ref[6, rows, lanes])
            inv = 1.0 / dist
            ubar = [jnp.zeros((8, 128), F32) for _ in range(3)]
            plain = jnp.zeros((8, 128), F32)
            tilted = jnp.zeros((8, 128), F32)
            for b in range(NB):
                value, off = terms[b]
                picked = [
                    jnp.take_along_axis(g_ref[f, 8 * b : 8 * b + 8, lanes], kind, axis=0) for f in range(4)
                ]
                bar = picked[0]
                for c in range(3):
                    bar = bar + unit[c] * picked[c + 1]
                    ubar[c] = ubar[c] + value * picked[c + 1]
                bar = bar * value
                plain = plain + bar
                tilted = tilted + bar * off
            along = ubar[0] * unit[0] + ubar[1] * unit[1] + ubar[2] * unit[2]
            dist_bar = tilted * (-1.0 / CENTRE_STEP**2) - along * inv
            radial = dist * (2.0 * (-0.25 * plain) + dist_bar * inv)
            for c in range(3):
                bar = ubar[c] * inv + unit[c] * radial
                rbar_ref[c, rows, lanes] = bar
                own[c] = own[c] + bar
        for c in range(3):
            own_out[c : c + 1, lanes] = -jnp.sum(own[c], axis=0, keepdims=True)
        return carry

    lax.fori_loop(0, tiles, slots, 0)

    block_rows = 24
    rows_high = iota((block_rows, atoms), 0)
    rows_low = iota((128, atoms), 0)

    def scatter(s, total):
        index = jnp.maximum(nbr_ref[pl.ds(s, 1), :], 0)
        at_high = rows_high == (index >> 7)
        at_low = jnp.where(rows_low == (index & 127), 1.0, 0.0).astype(BF16)
        pieces = []
        for c in range(3):
            value = rbar_ref[c, pl.ds(s, 1), :]
            high = value.astype(BF16).astype(F32)
            pieces.append(jnp.where(at_high, high, 0.0))
            pieces.append(jnp.where(at_high, value - high, 0.0))
        left = jnp.concatenate(pieces, axis=0).astype(BF16)
        return total + mm(left, at_low, NT)

    even = (where_ref[1] & 1) == 0
    total = lax.fori_loop(0, nbr_ref.shape[0], scatter, jnp.zeros((6 * block_rows, 128), F32), unroll=16)
    for c in range(3):
        at = 2 * block_rows * c
        table = total[at : at + block_rows] + total[at + block_rows : at + 2 * block_rows]
        for j in range(tiles):
            lanes = pl.ds(128 * j, 128)
            own_out[c : c + 1, lanes] = own_out[c : c + 1, lanes] + table[j : j + 1]
        for i in range(3):
            for h in range(2):
                lanes = slice(128 * h, 128 * h + 128)
                prev, mid, after = (table[row : row + 1] for row in (tiles + 2 * (3 * i + j) + h for j in range(3)))
                mid_out[i, c : c + 1, lanes] = mid
                first_out[i, c : c + 1, lanes] = jnp.where(even, after, prev)
                second_out[i, c : c + 1, lanes] = jnp.where(even, prev, after)


def ewald_kernel(
    grid,
    where_ref,
    pos_ref,
    nh_ref,
    nl_ref,
    fh_ref,
    fl_ref,
    x_ref,
    zy_ref,
    neutral_ref,
    own_ref,
    out_ref,
    high_ref,
    low_ref,
    z_ref,
    dz_ref,
    y_ref,
    dy_ref,
):
    extent_x, extent_y = grid
    core = where_ref[0] & 1
    neutral = neutral_ref[...]
    turn_x, rate_x, turn_z, turn_y, rate_y = waves(grid, where_ref, pos_ref)
    first = core == 0
    coefficients = [
        (jnp.where(first, nh_ref[...], fh_ref[...]), jnp.where(first, nl_ref[...], fl_ref[...]), slice(0, 256)),
        (jnp.where(first, fh_ref[...], nh_ref[...]), jnp.where(first, fl_ref[...], nl_ref[...]), slice(256, 512)),
    ]

    def total(c, functions, high_ref, low_ref):
        spread = None
        for high, low, at in coefficients:
            near, rest = high_ref[at, :], low_ref[at, :]
            term = mm(high, near) + (mm(low, near) + mm(high, rest))
            spread = term if spread is None else spread + term
        field = None
        for k in range(XF):
            term = functions[k : k + 1, :] * spread[32 * k : 32 * k + 32]
            field = term if field is None else field + term
        out_ref[c : c + 1, :] = own_ref[c : c + 1, :] + 2.0 * jnp.sum(neutral * field, axis=0, keepdims=True)

    total(0, cos_turns(turn_x + 0.25) * rate_x, zy_ref.at[0], zy_ref.at[1])
    z_ref[...] = cos_turns(turn_z)
    dz_ref[...] = cos_turns(turn_z + 0.25)
    y_ref[...] = cos_turns(turn_y)
    dy_ref[...] = cos_turns(turn_y + 0.25) * rate_y
    for c in (2, 1):
        for at in range(2 * LZ):
            turned = dz_ref[at : at + 1, :]
            if c == 2:
                value = (TWO_PI / BOX_HEIGHT * (at // 2 + 1)) * turned * y_ref[...]
            else:
                value = z_ref[at : at + 1, :] * dy_ref[...] - (0.5 * TWO_PI / extent_y) * turned * y_ref[...]
            high, low = parts(value)
            high_ref[64 * at : 64 * at + 64, :] = high
            low_ref[64 * at : 64 * at + 64, :] = low
        total(c, x_ref, high_ref, low_ref)


def finish_kernel(base_ref, mid_ref, first_ref, second_ref, ghost_ref, out_ref, back_ref, sems):
    atoms = base_ref.shape[1]
    copies = [
        pltpu.make_async_copy(ref, back_ref.at[n], sems.at[n]) for n, ref in enumerate((mid_ref, first_ref, second_ref))
    ]
    for copy in copies:
        copy.start()
    for copy in copies:
        copy.wait()
    returned = back_ref[0] + back_ref[1] + back_ref[2]
    high = returned.astype(BF16).astype(F32)
    rest = returned - high
    middle = rest.astype(BF16).astype(F32)
    split = jnp.concatenate([high, middle, rest - middle, jnp.zeros((7, 256), F32)], axis=0).astype(BF16)
    at = jnp.where(iota((atoms, 256), 0) == ghost_ref[...], 1.0, 0.0).astype(BF16)
    spread = mm(split, at, NT)
    out_ref[...] = -(base_ref[...] + ((spread[0:3] + spread[3:6]) + spread[6:9]))


def swapped(array, axis, far):
    n = lax.axis_size(axis)
    pairs = [(i, (i + (1 if i % 2 else -1)) % n if far else i ^ 1) for i in range(n)]
    return lax.ppermute(array, axis, pairs)


def along_z(array, flip):
    first, second = lax.axis_size("gx"), lax.axis_size("gy")
    pairs = []
    for device in range(first * second):
        u, v = divmod(device, second)
        z = (v // 16 * 4 + u // 2) ^ flip
        pairs.append((device, (z % 4 * 2 + u % 2) * second + z // 4 * 16 + v % 16))
    return lax.ppermute(array, AXES, pairs)


def across_plane(array):
    planes = [list(range(16 * k, 16 * k + 16)) for k in range(lax.axis_size("gy") // 16)]
    return lax.all_to_all(array, "gy", 0, 0, tiled=True, axis_index_groups=planes)


def reduced(keep, send):
    keep = keep + swapped(send, "gx", False)
    got = across_plane(keep.reshape(16, -1, 128))
    return sum((got[k] for k in range(1, 16)), got[0])


def shards(
    positions,
    species,
    neighbours,
    ghost_index,
    wave_index,
    embedding,
    radial_weight,
    message_weight,
    scalar_weight,
    vector_weight,
    readout_hidden,
    readout_vector,
    charge_weight,
):
    atoms = positions.shape[1]
    extents = lax.axis_size("gx"), lax.axis_size("gy")
    atoms_all = atoms * extents[0] * extents[1]
    where = jnp.stack([lax.axis_index("gx"), lax.axis_index("gy")])
    kinds = species[None]
    ghosts = ghost_index[None]

    (border,) = call(border_kernel, [((4, 256), F32)], [pltpu.VMEM((8, atoms), F32)], spaces="vvv", vmem=4)(positions, kinds, ghosts)
    even = [(where[axis] & 1) == 0 for axis in range(2)]
    second, first = swapped(border, "gy", True), swapped(border, "gy", False)
    fx, zy, unit, pair, pair_t, embed, readout = call(
        functools.partial(prepare_kernel, extents),
        [
            ((XROWS, atoms), F32),
            ((2, 128 * LZ, atoms), BF16),
            ((LZ, XROWS, 128), F32),
            ((2, 128, 64), F32),
            ((2, 64, 128), F32),
            ((128, 8), F32),
            ((128, 8), F32),
        ],
        spaces="svvvvv",
        vmem=16,
        flops=10**9,
        nbytes=2 * 10**6,
    )(where, positions, embedding, radial_weight, message_weight, readout_vector[None])
    second, first, zy = lax.optimization_barrier((second, first, zy))
    mid = jnp.stack([jnp.where(even[1], second, first), border, jnp.where(even[1], first, second)])
    second, first = swapped(mid, "gx", True), swapped(mid, "gx", False)

    nbr = neighbours.T
    charge_t = charge_weight.T
    charge, hbar, slope, vsum, geo, keep, send = call(
        forward_kernel,
        [
            ((40, atoms), F32),
            ((128, atoms), F32),
            ((128, atoms), F32),
            ((3, 128, atoms), F32),
            ((7, 32, atoms), F32),
            ((HALF, 128), F32),
            ((HALF, 128), F32),
        ],
        [
            pltpu.VMEM((4, 24, 128), F32),
            pltpu.VMEM((4, 64, atoms), F32),
            pltpu.VMEM((SLAB, atoms), BF16),
            pltpu.VMEM((SLAB, atoms), BF16),
            pltpu.VMEM((3, 3, 4, 256), F32),
            pltpu.SemaphoreType.DMA((3,)),
        ],
        spaces="svvaaa" + "v" * 11,
        vmem=16,
        flops=5 * 10**9,
        nbytes=4 * 10**6,
    )(
        where,
        positions,
        kinds,
        mid,
        first,
        second,
        nbr,
        embed,
        pair,
        scalar_weight,
        vector_weight,
        readout_hidden,
        readout,
        charge_t,
        fx,
        zy,
        unit,
    )

    keep = reduced(keep, send)
    keep = keep + along_z(keep, 1)
    got = along_z(keep, 2)
    keep, waves_late, charge_late = lax.optimization_barrier((keep, wave_index, charge_t))
    table, weight = call(
        functools.partial(later_kernel, extents, atoms_all),
        [((4, 40, 128), F32), ((128, 32), F32)],
        spaces="vv",
        vmem=16,
        flops=10**9,
        nbytes=2 * 10**6,
    )(waves_late, charge_late)
    got, table, weight = lax.optimization_barrier((got, table, weight))
    keep = keep + got
    keep = keep + along_z(keep, 6)
    near = across_plane(jnp.broadcast_to(keep, (16,) + keep.shape)).reshape(-1, 128)
    far = swapped(near, "gx", False)
    nh, nl, potential, overlap = call(
        functools.partial(near_kernel, atoms_all),
        [((SLAB, 256), BF16), ((SLAB, 256), BF16), ((32, atoms), F32), ((32, 128), F32)],
        spaces="svvvv",
        vmem=16,
        flops=10**9,
        nbytes=2 * 10**6,
    )(where, near, table, fx, zy)
    far, potential = lax.optimization_barrier((far, potential))

    site, neutral, fh, fl, own, g_mid, g_first, g_second = call(
        functools.partial(backward_kernel, atoms_all),
        [
            ((1, atoms), F32),
            ((32, atoms), F32),
            ((SLAB, 256), BF16),
            ((SLAB, 256), BF16),
            ((3, atoms), F32),
            ((3, 3, 256), F32),
            ((3, 3, 256), F32),
            ((3, 3, 256), F32),
        ],
        [pltpu.VMEM((4, 64, atoms), F32), pltpu.VMEM((3, 32, atoms), F32)],
        spaces="s" + "v" * 16,
        vmem=16,
        flops=5 * 10**9,
        nbytes=4 * 10**6,
    )(
        where,
        far,
        table,
        fx,
        zy,
        potential,
        overlap,
        charge,
        hbar,
        slope,
        vsum,
        geo,
        nbr,
        scalar_weight,
        vector_weight,
        weight,
        pair_t,
    )

    second, first = swapped(g_second, "gy", True), swapped(g_first, "gy", False)
    (base,) = call(
        functools.partial(ewald_kernel, extents),
        [((3, atoms), F32)],
        [pltpu.VMEM((128 * LZ, atoms), BF16)] * 2 + [pltpu.VMEM((rows, atoms), F32) for rows in (8, 8, 64, 64)],
        spaces="s" + "v" * 9,
        vmem=16,
        flops=5 * 10**9,
        nbytes=4 * 10**6,
    )(where, positions, nh, nl, fh, fl, fx, zy, neutral, own)
    first, second, base = lax.optimization_barrier((first, second, base))
    column = g_mid + first + second
    second = swapped(jnp.where(even[0], column[0], column[2]), "gx", True)
    first = swapped(jnp.where(even[0], column[2], column[0]), "gx", False)
    (forces,) = call(
        finish_kernel,
        [((3, atoms), F32)],
        [pltpu.VMEM((3, 3, 256), F32), pltpu.SemaphoreType.DMA((3,))],
        spaces="vaaav",
        vmem=4,
    )(base, column[1], first, second, ghosts)
    return forces, site[0]


def solution(mesh):
    return jax.shard_map(
        shards,
        mesh=mesh,
        in_specs=(
            P(None, ("gx", "gy")),
            P(("gx", "gy")),
            P(("gx", "gy"), None),
            P(("gx", "gy")),
            P(),
            P(),
            P(),
            P(),
            P(),
            P(),
            P(),
            P(),
            P(),
        ),
        out_specs=(P(None, ("gx", "gy")), P(("gx", "gy"))),
        check_vma=False,
    )
```

```python
import functools

import jax
import jax.numpy as jnp
from jax import lax
from jax.experimental import pallas as pl
from jax.experimental.pallas import tpu as pltpu
from jax.sharding import PartitionSpec as P

NB = 8
NS = 8
HIGHEST = lax.Precision.HIGHEST
TWO_PI = 6.283185307179586
BOX_HEIGHT = 4.0
SPLITTING = 2.5
SOFTENING = 0.01
CENTRE_STEP = 0.3
AXES = ("gx", "gy")

HX = 9
LZ = 4
NY = 32
XF = 2 * HX - 1
XROWS = 24
SLAB = XF * 32
UNIT_ROW = 2 * SLAB
TOTAL_ROW = UNIT_ROW + 2 * XROWS
HALF = TOTAL_ROW + 16

F32 = jnp.float32
BF16 = jnp.bfloat16
NT = (((1,), (1,)), ((), ()))
NN = (((1,), (0,)), ((), ()))


def mm(a, b, dims=NN, precision=None):
    return lax.dot_general(a, b, dims, precision=precision, preferred_element_type=F32)


def parts(x):
    high = x.astype(BF16)
    return high, (x - high.astype(F32)).astype(BF16)


def mm3(a, b, dims=NN):
    a_high, a_low = parts(a)
    b_high, b_low = parts(b)
    return mm(a_high, b_high, dims) + (mm(a_low, b_high, dims) + mm(a_high, b_low, dims))


def cos_turns(t):
    r = t - jnp.floor(t + 0.5)
    s = (0.25 - jnp.abs(r)) * TWO_PI
    q = s * s
    p = -2.5052108e-08 + q * 1.6059044e-10
    p = 2.7557319e-06 + q * p
    p = -1.9841270e-04 + q * p
    p = 8.3333333e-03 + q * p
    p = -1.6666667e-01 + q * p
    return s + s * (q * p)


def silu_parts(x):
    gate = 1.0 / (1.0 + jnp.exp(-x))
    return x * gate, gate * (1.0 + x * (1.0 - gate))


def iota(shape, dim):
    return lax.broadcasted_iota(jnp.int32, shape, dim)


def call(kernel, outs, scratch=(), spaces="", flops=0, nbytes=0, vmem=56):
    known = {"s": pltpu.SMEM, "v": pltpu.VMEM, "a": pl.ANY, "h": pltpu.HBM}
    return pl.pallas_call(
        kernel,
        in_specs=[pl.BlockSpec(memory_space=known[letter]) for letter in spaces],
        out_shape=[jax.ShapeDtypeStruct(s, d) for s, d in outs],
        scratch_shapes=list(scratch),
        compiler_params=pltpu.CompilerParams(vmem_limit_bytes=vmem * 2**20),
        cost_estimate=pl.CostEstimate(flops=flops, bytes_accessed=nbytes, transcendentals=0),
    )


def border_kernel(pos_ref, species_ref, ghost_ref, out_ref, tab_ref):
    atoms = pos_ref.shape[1]
    tab_ref[0:3, :] = pos_ref[...]
    tab_ref[3:4, :] = species_ref[...].astype(F32)
    for part in range(ghost_ref.shape[1] // 128):
        lanes = pl.ds(128 * part, 128)
        index = jnp.broadcast_to(ghost_ref[:, lanes], (8, 128))
        high, low = index >> 7, index & 127
        value = jnp.zeros((8, 128), F32)
        for block in range(atoms // 128):
            source = tab_ref[:, pl.ds(128 * block, 128)]
            value = jnp.where(high == block, jnp.take_along_axis(source, low, axis=1), value)
        out_ref[:, lanes] = value[0:4]


def waves(grid, where_ref, pos_ref):
    extent_x, extent_y = grid
    atoms = pos_ref.shape[1]
    u, v = where_ref[0], where_ref[1]
    x, y, z = pos_ref[0:1, :], pos_ref[1:2, :], pos_ref[2:3, :]

    row = iota((XROWS, atoms), 0)
    order = jnp.where(row < HX, row, row - (HX - 1))
    whole = lax.rem(order * u, extent_x).astype(F32)
    order = order.astype(F32)
    turn_x = (order * x + whole) / extent_x - jnp.where(row < HX, 0.0, 0.25)
    rate_x = jnp.where(row < XF, order * (TWO_PI / extent_x), 0.0)

    row = iota((2 * LZ, atoms), 0)
    whole = lax.rem(v, 2 * extent_y).astype(F32)
    turn_z = ((row >> 1) + 1).astype(F32) * z * (1.0 / BOX_HEIGHT) - (y + whole) * (0.5 / extent_y)
    turn_z = turn_z - 0.25 * (row & 1).astype(F32)

    row = iota((2 * NY, atoms), 0)
    twice = 2 * (row & (NY - 1)) + 1
    whole = lax.rem(twice * v, 2 * extent_y).astype(F32)
    twice = twice.astype(F32)
    turn_y = (twice * y + whole) * (0.5 / extent_y) - jnp.where(row < NY, 0.0, 0.25)
    return turn_x, rate_x, turn_z, turn_y, twice * (0.5 * TWO_PI / extent_y)


def prepare_kernel(
    grid,
    where_ref,
    pos_ref,
    embed_ref,
    radial_ref,
    message_ref,
    readout_ref,
    x_out,
    zy_out,
    unit_out,
    weight_out,
    weight_t_out,
    embed_out,
    readout_out,
):
    turn_x, _, turn_z, turn_y, _ = waves(grid, where_ref, pos_ref)
    fx = jnp.where(iota(turn_x.shape, 0) < XF, cos_turns(turn_x), 0.0)
    fz, fy = cos_turns(turn_z), cos_turns(turn_y)
    x_out[...] = fx

    for l in range(LZ):
        zy = jnp.concatenate([fz[2 * l : 2 * l + 1] * fy, fz[2 * l + 1 : 2 * l + 2] * fy], axis=0)
        high, low = parts(zy)
        zy_out[0, 128 * l : 128 * l + 128] = high
        zy_out[1, 128 * l : 128 * l + 128] = low
        unit_out[l] = mm(fx, zy, NT, HIGHEST)

    embed = embed_ref[...].T
    message = mm(message_ref[...].T, embed, NN, HIGHEST)
    embed_out[...] = embed
    readout_out[...] = jnp.broadcast_to(readout_ref[...], (8, 128)).T
    col = iota((NB, 64), 1)
    sub = iota((NB, 64), 0)
    pick_b = ((col >> 3) == sub).astype(F32)
    pick_s = ((col & 7) == sub).astype(F32)
    spread = mm(message, pick_s, NN, HIGHEST)
    radial = radial_ref[...].T
    channels = message.shape[0]
    for which in range(2):
        weight = mm(radial[which * channels : (which + 1) * channels], pick_b, NN, HIGHEST) * spread
        weight_out[which] = weight
        weight_t_out[which] = weight.T


def later_kernel(
    grid,
    atoms_all,
    wave_ref,
    charge_ref,
    table_out,
    charge_out,
):
    extent_x, extent_y = grid

    step = wave_ref.shape[1]
    order = iota((40, step), 0)
    along_x, along_y, along_z = wave_ref[0:1, :], wave_ref[1:2, :], wave_ref[2:3, :]
    matches_z = ((order & 3) + 1 == along_z) & (order < HX * LZ)
    plus = matches_z & ((order >> 2) == along_x)
    minus = matches_z & ((order >> 2) == -along_x) & (order >= LZ)
    lanes = iota((NY, step), 0)
    up = (lanes == along_y).astype(F32).astype(BF16)
    down = (-lanes - 1 == along_y).astype(F32).astype(BF16)
    both = jnp.concatenate([up] * 4 + [down] * 4, axis=0)
    plus = mm(plus.astype(F32).astype(BF16), both, NT)
    minus = mm(minus.astype(F32).astype(BF16), both, NT)
    order = iota((40, 128), 0)
    lanes = iota((40, 128), 1)
    wave_b = (lanes & (NY - 1)).astype(F32)
    kx = (order >> 2).astype(F32) * (TWO_PI / extent_x)
    kz = ((order & 3) + 1).astype(F32) * (TWO_PI / BOX_HEIGHT)

    def weights(ky):
        squared = kx * kx + ky * ky + kz * kz
        return jnp.exp(-squared / (4.0 * SPLITTING**2)) / squared / atoms_all

    green_up = weights(wave_b * (TWO_PI / extent_y))
    green_down = weights((wave_b + 1.0) * (TWO_PI / extent_y))
    pp, pm = green_up * plus[:, 0:128], green_down * plus[:, 128:256]
    mp, mn = green_up * minus[:, 0:128], green_down * minus[:, 128:256]
    quarter = lanes >> 5
    sign_t = jnp.where((quarter == 1) | (quarter == 2), 1.0, -1.0)
    sign_st = jnp.where((quarter & 1) == 1, 1.0, -1.0)
    sign_s = jnp.where(quarter >= 2, 1.0, -1.0)
    table_out[0] = (pp + pm) + (mp + mn)
    table_out[1] = sign_t * ((pp - pm) + (mp - mn))
    table_out[2] = sign_st * ((pp - pm) - (mp - mn))
    table_out[3] = sign_s * ((pp + pm) - (mp + mn))

    charge_out[...] = charge_ref[...].T


def basis_terms(dist, rho, live):
    envelope = jnp.exp(-0.25 * rho) * live
    out = []
    for b in range(NB):
        off = dist - CENTRE_STEP * b
        out.append((jnp.exp(off * off * (-0.5 / CENTRE_STEP**2)) * envelope, off))
    return out


def forward_kernel(
    where_ref,
    pos_ref,
    species_ref,
    mid_ref,
    first_ref,
    second_ref,
    nbr_ref,
    embed_ref,
    pair_ref,
    scalar_ref,
    vector_ref,
    hidden_ref,
    readout_ref,
    weight_ref,
    x_ref,
    zy_ref,
    unit_ref,
    charge_out,
    hbar_out,
    slope_out,
    vsum_out,
    geo_out,
    keep_out,
    send_out,
    tab_ref,
    moment_ref,
    qh_ref,
    ql_ref,
    halo_ref,
    sems,
):
    atoms = pos_ref.shape[1]
    tiles = atoms // 128
    copies = [
        pltpu.make_async_copy(ref, halo_ref.at[n], sems.at[n]) for n, ref in enumerate((mid_ref, first_ref, second_ref))
    ]
    for copy in copies:
        copy.start()
    for c in range(3):
        for j in range(tiles):
            tab_ref[c, j : j + 1, :] = pos_ref[c : c + 1, pl.ds(128 * j, 128)]
    for j in range(tiles):
        tab_ref[3, j : j + 1, :] = species_ref[:, pl.ds(128 * j, 128)].astype(F32)
    for copy in copies:
        copy.wait()
    even = (where_ref[0] & 1) == 0
    for j in range(3):
        first, second = halo_ref[1, j], halo_ref[2, j]
        prev, after = jnp.where(even, second, first), jnp.where(even, first, second)
        for i, block in enumerate((prev, halo_ref[0, j], after)):
            shifts = (i - 1.0, j - 1.0, 0.0, 0.0)
            for c in range(4):
                for h in range(2):
                    at = tiles + 2 * (3 * i + j) + h
                    tab_ref[c, at : at + 1, :] = block[c : c + 1, 128 * h : 128 * h + 128] + shifts[c]

    def lane_tile(t, carry):
        lanes = pl.ds(pl.multiple_of(t * 128, 128), 128)
        for tile in range(4):
            index = nbr_ref[pl.ds(8 * tile, 8), lanes]
            live = (index >= 0).astype(F32)
            index = jnp.maximum(index, 0)
            high, low = index >> 7, index & 127
            value = [jnp.zeros((8, 128), F32) for _ in range(4)]
            for block in range(tiles + 18):
                if block // 2 == tiles // 2 + 4:
                    continue
                here = high == block
                for c in range(4):
                    source = jnp.broadcast_to(tab_ref[c, block : block + 1, :], (8, 128))
                    value[c] = jnp.where(here, jnp.take_along_axis(source, low, axis=1), value[c])
            rx, ry, rz = (value[c] - pos_ref[c : c + 1, lanes] for c in range(3))
            rho = rx * rx + ry * ry + rz * rz
            dist = jnp.sqrt(rho + SOFTENING)
            inv = 1.0 / dist
            rows = pl.ds(8 * tile, 8)
            geo_out[0, rows, lanes] = rx * inv
            geo_out[1, rows, lanes] = ry * inv
            geo_out[2, rows, lanes] = rz * inv
            geo_out[3, rows, lanes] = dist
            geo_out[4, rows, lanes] = rho
            geo_out[5, rows, lanes] = value[3]
            geo_out[6, rows, lanes] = live
        dist = geo_out[3, :, lanes]
        terms = basis_terms(dist, geo_out[4, :, lanes], geo_out[6, :, lanes])
        kind = geo_out[5, :, lanes]
        for f in range(4):
            for b in range(NB):
                value = terms[b][0] if f == 0 else terms[b][0] * geo_out[f - 1, :, lanes]
                rows = []
                for s in range(NS):
                    chosen = jnp.where(kind == float(s), value, 0.0)
                    rows.append((chosen[0:8] + chosen[8:16]) + (chosen[16:24] + chosen[24:32]))
                for step in (4, 2, 1):
                    here = (iota((8, 128), 0) & step) == 0
                    rows = [
                        jnp.where(here, one + pltpu.roll(one, 8 - step, 0), two + pltpu.roll(two, step, 0))
                        for one, two in zip(rows[: len(rows) // 2], rows[len(rows) // 2 :])
                    ]
                moment_ref[f, 8 * b : 8 * b + 8, lanes] = rows[0]
        return carry

    lax.fori_loop(0, tiles, lane_tile, 0, unroll=2)

    def gathered(f):
        return mm3(pair_ref[0 if f == 0 else 1], moment_ref[f])

    scalar_sum = gathered(0)
    norm = None
    for c in range(3):
        vector = gathered(c + 1)
        vsum_out[c] = vector
        norm = vector * vector if norm is None else norm + vector * vector
    update = mm3(scalar_ref[...].T, scalar_sum) + mm3(vector_ref[...].T, norm)
    feature = jnp.zeros_like(update)
    kinds = species_ref[...]
    for s in range(NS):
        feature = jnp.where(kinds == s, embed_ref[:, s : s + 1], feature)
    act, slope = silu_parts(update)
    slope_out[...] = slope
    hidden = feature + act
    act, slope = silu_parts(mm3(hidden_ref[...].T, hidden))
    readout = readout_ref[:, 0:1]
    charge_out[32:33, :] = jnp.sum(act * readout, axis=0, keepdims=True)
    hbar_out[...] = mm3(hidden_ref[...], slope * readout)
    charges = mm3(weight_ref[...], hidden)
    charge_out[0:32, :] = charges
    charge_out[33:40, :] = jnp.zeros((7, atoms), F32)

    total = jnp.sum(charges, axis=1, keepdims=True)
    local = total * (1.0 / atoms)
    centred = charges - local
    for k in range(XF):
        high, low = parts(centred * x_ref[k : k + 1, :])
        qh_ref[32 * k : 32 * k + 32, :] = high
        ql_ref[32 * k : 32 * k + 32, :] = low
    high, low = qh_ref[...], ql_ref[...]
    core = where_ref[0] & 1
    for out, half in ((send_out, 1 - core), (keep_out, core)):
        near, rest = (zy_ref[part, pl.ds(pl.multiple_of(256 * half, 256), 256), :] for part in range(2))
        slabs = mm(high, near, NT) + (mm(low, near, NT) + mm(high, rest, NT))
        for n in range(2):
            unit = unit_ref[2 * half + n]
            for k in range(XF):
                at = SLAB * n + 32 * k
                value = slabs[32 * k : 32 * k + 32, 128 * n : 128 * n + 128]
                out[at : at + 32, :] = value + local * unit[k : k + 1]
            out[UNIT_ROW + XROWS * n : UNIT_ROW + XROWS * (n + 1), :] = unit
        out[TOTAL_ROW:HALF, :] = jnp.where(iota((16, 128), 1) < 64, total[0:16], total[16:32])


def quarters(x, which):
    lane = iota(x.shape, 1)
    if which == 2:
        return pltpu.roll(x, 64, 1)
    even = ((lane >> 5) & 1) == 0
    if which == 1:
        return jnp.where(even, pltpu.roll(x, 96, 1), pltpu.roll(x, 32, 1))
    return jnp.where(even, pltpu.roll(x, 32, 1), pltpu.roll(x, 96, 1))


def contribution(half, ref, table_ref, x_ref, zy_ref, vh_out, vl_out, atoms_all):
    ends = ref[TOTAL_ROW:HALF, :]
    mean = jnp.concatenate([ends[:, 0:1], ends[:, 64:65]], axis=0) * (1.0 / atoms_all)

    def put(n, k, value):
        rows = pl.ds(pl.multiple_of(k * 32, 32), 32)
        high, low = parts(value)
        vh_out[rows, 128 * n : 128 * n + 128] = high
        vl_out[rows, 128 * n : 128 * n + 128] = low

    def tile_of(n, k):
        unit = ref[pl.ds(UNIT_ROW + XROWS * n + k, 1), :]
        rows = pl.ds(pl.multiple_of(SLAB * n + k * 32, 32), 32)
        return ref[rows, :] - mean * unit, unit

    overlap = jnp.zeros((32, 128), F32)
    for n in range(2):
        cos_tile, unit = tile_of(n, 0)
        g0, gt = (table_ref[t, pl.ds(2 * half + n, 1), :] for t in range(2))
        value = g0 * cos_tile + gt * quarters(cos_tile, 3)
        overlap = overlap + value * unit
        put(n, 0, value)

    def mix(a, overlap):
        for n in range(2):
            cos_tile, cos_unit = tile_of(n, a)
            sin_tile, sin_unit = tile_of(n, a + HX - 1)
            g0, gt, gst, gs = (table_ref[t, pl.ds(a * LZ + 2 * half + n, 1), :] for t in range(4))
            value = (g0 * cos_tile + gt * quarters(cos_tile, 3)) + (
                gst * quarters(sin_tile, 1) + gs * quarters(sin_tile, 2)
            )
            overlap = overlap + value * cos_unit
            put(n, a, value)
            value = (g0 * sin_tile + gt * quarters(sin_tile, 3)) - (
                gst * quarters(cos_tile, 1) + gs * quarters(cos_tile, 2)
            )
            overlap = overlap + value * sin_unit
            put(n, a + HX - 1, value)
        return overlap

    overlap = lax.fori_loop(1, HX, mix, overlap, unroll=8)
    at = pl.ds(pl.multiple_of(256 * half, 256), 256)
    high, low = zy_ref[0, at, :], zy_ref[1, at, :]
    spread = mm(vh_out[...], high) + (mm(vl_out[...], high) + mm(vh_out[...], low))
    potential = jnp.zeros((32, zy_ref.shape[2]), F32)
    for k in range(XF):
        potential = potential + x_ref[k : k + 1, :] * spread[32 * k : 32 * k + 32]
    return mean, potential, overlap


def near_kernel(
    atoms_all, where_ref, near_ref, table_ref, x_ref, zy_ref, vh_out, vl_out, potential_out, overlap_out
):
    half = where_ref[0] & 1
    _, potential, overlap = contribution(half, near_ref, table_ref, x_ref, zy_ref, vh_out, vl_out, atoms_all)
    potential_out[...] = potential
    overlap_out[...] = overlap


def backward_kernel(
    atoms_all,
    where_ref,
    far_ref,
    table_ref,
    x_ref,
    zy_ref,
    potential_ref,
    overlap_ref,
    charge_ref,
    hbar_ref,
    slope_ref,
    vsum_ref,
    geo_ref,
    nbr_ref,
    scalar_ref,
    vector_ref,
    weight_ref,
    pair_ref,
    site_out,
    neutral_out,
    vh_out,
    vl_out,
    own_out,
    mid_out,
    first_out,
    second_out,
    g_ref,
    rbar_ref,
):
    atoms = nbr_ref.shape[1]
    tiles = atoms // 128
    half = 1 - (where_ref[0] & 1)
    mean, potential, overlap = contribution(half, far_ref, table_ref, x_ref, zy_ref, vh_out, vl_out, atoms_all)
    potential = potential + potential_ref[...]
    overlap = overlap + overlap_ref[...]
    potential_mean = jnp.sum(overlap, axis=1, keepdims=True) * (1.0 / atoms_all)
    neutral = charge_ref[0:32, :] - mean
    neutral_out[...] = neutral
    site_out[...] = charge_ref[32:33, :] + jnp.sum(neutral * potential, axis=0, keepdims=True)
    charge_bar = 2.0 * (potential - potential_mean)
    update_bar = (hbar_ref[...] + mm3(weight_ref[...], charge_bar)) * slope_ref[...]
    scalar_bar = mm3(scalar_ref[...], update_bar)
    norm_bar = 2.0 * mm3(vector_ref[...], update_bar)
    g_ref[0] = mm3(pair_ref[0], scalar_bar)
    for c in range(3):
        g_ref[c + 1] = mm3(pair_ref[1], vsum_ref[c] * norm_bar)

    def slots(t, carry):
        lanes = pl.ds(pl.multiple_of(t * 128, 128), 128)
        own = [jnp.zeros((8, 128), F32) for _ in range(3)]
        for tile in range(4):
            rows = pl.ds(8 * tile, 8)
            unit = [geo_ref[c, rows, lanes] for c in range(3)]
            dist = geo_ref[3, rows, lanes]
            kind = geo_ref[5, rows, lanes].astype(jnp.int32)
            terms = basis_terms(dist, geo_ref[4, rows, lanes], geo_ref[6, rows, lanes])
            inv = 1.0 / dist
            ubar = [jnp.zeros((8, 128), F32) for _ in range(3)]
            plain = jnp.zeros((8, 128), F32)
            tilted = jnp.zeros((8, 128), F32)
            for b in range(NB):
                value, off = terms[b]
                picked = [
                    jnp.take_along_axis(g_ref[f, 8 * b : 8 * b + 8, lanes], kind, axis=0) for f in range(4)
                ]
                bar = picked[0]
                for c in range(3):
                    bar = bar + unit[c] * picked[c + 1]
                    ubar[c] = ubar[c] + value * picked[c + 1]
                bar = bar * value
                plain = plain + bar
                tilted = tilted + bar * off
            along = ubar[0] * unit[0] + ubar[1] * unit[1] + ubar[2] * unit[2]
            dist_bar = tilted * (-1.0 / CENTRE_STEP**2) - along * inv
            radial = dist * (2.0 * (-0.25 * plain) + dist_bar * inv)
            for c in range(3):
                bar = ubar[c] * inv + unit[c] * radial
                rbar_ref[c, rows, lanes] = bar
                own[c] = own[c] + bar
        for c in range(3):
            own_out[c : c + 1, lanes] = -jnp.sum(own[c], axis=0, keepdims=True)
        return carry

    lax.fori_loop(0, tiles, slots, 0)

    block_rows = 24
    rows_high = iota((block_rows, atoms), 0)
    rows_low = iota((128, atoms), 0)

    def scatter(s, total):
        index = jnp.maximum(nbr_ref[pl.ds(s, 1), :], 0)
        at_high = rows_high == (index >> 7)
        at_low = jnp.where(rows_low == (index & 127), 1.0, 0.0).astype(BF16)
        pieces = []
        for c in range(3):
            value = rbar_ref[c, pl.ds(s, 1), :]
            high = value.astype(BF16).astype(F32)
            pieces.append(jnp.where(at_high, high, 0.0))
            pieces.append(jnp.where(at_high, value - high, 0.0))
        left = jnp.concatenate(pieces, axis=0).astype(BF16)
        return total + mm(left, at_low, NT)

    even = (where_ref[1] & 1) == 0
    total = lax.fori_loop(0, nbr_ref.shape[0], scatter, jnp.zeros((6 * block_rows, 128), F32), unroll=16)
    for c in range(3):
        at = 2 * block_rows * c
        table = total[at : at + block_rows] + total[at + block_rows : at + 2 * block_rows]
        for j in range(tiles):
            lanes = pl.ds(128 * j, 128)
            own_out[c : c + 1, lanes] = own_out[c : c + 1, lanes] + table[j : j + 1]
        for i in range(3):
            for h in range(2):
                lanes = slice(128 * h, 128 * h + 128)
                prev, mid, after = (table[row : row + 1] for row in (tiles + 2 * (3 * i + j) + h for j in range(3)))
                mid_out[i, c : c + 1, lanes] = mid
                first_out[i, c : c + 1, lanes] = jnp.where(even, after, prev)
                second_out[i, c : c + 1, lanes] = jnp.where(even, prev, after)


def ewald_kernel(
    grid,
    where_ref,
    pos_ref,
    nh_ref,
    nl_ref,
    fh_ref,
    fl_ref,
    x_ref,
    zy_ref,
    neutral_ref,
    own_ref,
    out_ref,
    high_ref,
    low_ref,
    z_ref,
    dz_ref,
    y_ref,
    dy_ref,
):
    extent_x, extent_y = grid
    core = where_ref[0] & 1
    neutral = neutral_ref[...]
    turn_x, rate_x, turn_z, turn_y, rate_y = waves(grid, where_ref, pos_ref)
    first = core == 0
    coefficients = [
        (jnp.where(first, nh_ref[...], fh_ref[...]), jnp.where(first, nl_ref[...], fl_ref[...]), slice(0, 256)),
        (jnp.where(first, fh_ref[...], nh_ref[...]), jnp.where(first, fl_ref[...], nl_ref[...]), slice(256, 512)),
    ]

    def total(c, functions, high_ref, low_ref):
        spread = None
        for high, low, at in coefficients:
            near, rest = high_ref[at, :], low_ref[at, :]
            term = mm(high, near) + (mm(low, near) + mm(high, rest))
            spread = term if spread is None else spread + term
        field = None
        for k in range(XF):
            term = functions[k : k + 1, :] * spread[32 * k : 32 * k + 32]
            field = term if field is None else field + term
        out_ref[c : c + 1, :] = own_ref[c : c + 1, :] + 2.0 * jnp.sum(neutral * field, axis=0, keepdims=True)

    total(0, cos_turns(turn_x + 0.25) * rate_x, zy_ref.at[0], zy_ref.at[1])
    z_ref[...] = cos_turns(turn_z)
    dz_ref[...] = cos_turns(turn_z + 0.25)
    y_ref[...] = cos_turns(turn_y)
    dy_ref[...] = cos_turns(turn_y + 0.25) * rate_y
    for c in (2, 1):
        for at in range(2 * LZ):
            turned = dz_ref[at : at + 1, :]
            if c == 2:
                value = (TWO_PI / BOX_HEIGHT * (at // 2 + 1)) * turned * y_ref[...]
            else:
                value = z_ref[at : at + 1, :] * dy_ref[...] - (0.5 * TWO_PI / extent_y) * turned * y_ref[...]
            high, low = parts(value)
            high_ref[64 * at : 64 * at + 64, :] = high
            low_ref[64 * at : 64 * at + 64, :] = low
        total(c, x_ref, high_ref, low_ref)


def finish_kernel(base_ref, mid_ref, first_ref, second_ref, ghost_ref, out_ref, back_ref, sems):
    atoms = base_ref.shape[1]
    copies = [
        pltpu.make_async_copy(ref, back_ref.at[n], sems.at[n]) for n, ref in enumerate((mid_ref, first_ref, second_ref))
    ]
    for copy in copies:
        copy.start()
    for copy in copies:
        copy.wait()
    returned = back_ref[0] + back_ref[1] + back_ref[2]
    high = returned.astype(BF16).astype(F32)
    rest = returned - high
    middle = rest.astype(BF16).astype(F32)
    split = jnp.concatenate([high, middle, rest - middle, jnp.zeros((7, 256), F32)], axis=0).astype(BF16)
    at = jnp.where(iota((atoms, 256), 0) == ghost_ref[...], 1.0, 0.0).astype(BF16)
    spread = mm(split, at, NT)
    out_ref[...] = -(base_ref[...] + ((spread[0:3] + spread[3:6]) + spread[6:9]))


def swapped(array, axis, far):
    n = lax.axis_size(axis)
    pairs = [(i, (i + (1 if i % 2 else -1)) % n if far else i ^ 1) for i in range(n)]
    return lax.ppermute(array, axis, pairs)


def along_z(array, flip):
    first, second = lax.axis_size("gx"), lax.axis_size("gy")
    pairs = []
    for device in range(first * second):
        u, v = divmod(device, second)
        z = (v // 16 * 4 + u // 2) ^ flip
        pairs.append((device, (z % 4 * 2 + u % 2) * second + z // 4 * 16 + v % 16))
    return lax.ppermute(array, AXES, pairs)


def across_plane(array):
    planes = [list(range(16 * k, 16 * k + 16)) for k in range(lax.axis_size("gy") // 16)]
    return lax.all_to_all(array, "gy", 0, 0, tiled=True, axis_index_groups=planes)


def reduced(keep, send):
    keep = keep + swapped(send, "gx", False)
    got = across_plane(keep.reshape(16, -1, 128))
    return sum((got[k] for k in range(1, 16)), got[0])


def shards(
    positions,
    species,
    neighbours,
    ghost_index,
    wave_index,
    embedding,
    radial_weight,
    message_weight,
    scalar_weight,
    vector_weight,
    readout_hidden,
    readout_vector,
    charge_weight,
):
    atoms = positions.shape[1]
    extents = lax.axis_size("gx"), lax.axis_size("gy")
    atoms_all = atoms * extents[0] * extents[1]
    where = jnp.stack([lax.axis_index("gx"), lax.axis_index("gy")])
    kinds = species[None]
    ghosts = ghost_index[None]

    (border,) = call(border_kernel, [((4, 256), F32)], [pltpu.VMEM((8, atoms), F32)], spaces="vvv", vmem=4)(positions, kinds, ghosts)
    even = [(where[axis] & 1) == 0 for axis in range(2)]
    second, first = swapped(border, "gy", True), swapped(border, "gy", False)
    fx, zy, unit, pair, pair_t, embed, readout = call(
        functools.partial(prepare_kernel, extents),
        [
            ((XROWS, atoms), F32),
            ((2, 128 * LZ, atoms), BF16),
            ((LZ, XROWS, 128), F32),
            ((2, 128, 64), F32),
            ((2, 64, 128), F32),
            ((128, 8), F32),
            ((128, 8), F32),
        ],
        spaces="svvvvv",
        vmem=16,
        flops=10**9,
        nbytes=2 * 10**6,
    )(where, positions, embedding, radial_weight, message_weight, readout_vector[None])
    second, first, zy = lax.optimization_barrier((second, first, zy))
    mid = jnp.stack([jnp.where(even[1], second, first), border, jnp.where(even[1], first, second)])
    second, first = swapped(mid, "gx", True), swapped(mid, "gx", False)

    nbr = neighbours.T
    charge_t = charge_weight.T
    charge, hbar, slope, vsum, geo, keep, send = call(
        forward_kernel,
        [
            ((40, atoms), F32),
            ((128, atoms), F32),
            ((128, atoms), F32),
            ((3, 128, atoms), F32),
            ((7, 32, atoms), F32),
            ((HALF, 128), F32),
            ((HALF, 128), F32),
        ],
        [
            pltpu.VMEM((4, 24, 128), F32),
            pltpu.VMEM((4, 64, atoms), F32),
            pltpu.VMEM((SLAB, atoms), BF16),
            pltpu.VMEM((SLAB, atoms), BF16),
            pltpu.VMEM((3, 3, 4, 256), F32),
            pltpu.SemaphoreType.DMA((3,)),
        ],
        spaces="svvaaa" + "v" * 11,
        vmem=16,
        flops=5 * 10**9,
        nbytes=4 * 10**6,
    )(
        where,
        positions,
        kinds,
        mid,
        first,
        second,
        nbr,
        embed,
        pair,
        scalar_weight,
        vector_weight,
        readout_hidden,
        readout,
        charge_t,
        fx,
        zy,
        unit,
    )

    keep = reduced(keep, send)
    keep = keep + along_z(keep, 1)
    got = along_z(keep, 2)
    keep, waves_late, charge_late = lax.optimization_barrier((keep, wave_index, charge_t))
    table, weight = call(
        functools.partial(later_kernel, extents, atoms_all),
        [((4, 40, 128), F32), ((128, 32), F32)],
        spaces="vv",
        vmem=16,
        flops=10**9,
        nbytes=2 * 10**6,
    )(waves_late, charge_late)
    got, table, weight = lax.optimization_barrier((got, table, weight))
    keep = keep + got
    keep = keep + along_z(keep, 6)
    near = across_plane(jnp.broadcast_to(keep, (16,) + keep.shape)).reshape(-1, 128)
    far = swapped(near, "gx", False)
    nh, nl, potential, overlap = call(
        functools.partial(near_kernel, atoms_all),
        [((SLAB, 256), BF16), ((SLAB, 256), BF16), ((32, atoms), F32), ((32, 128), F32)],
        spaces="svvvv",
        vmem=16,
        flops=10**9,
        nbytes=2 * 10**6,
    )(where, near, table, fx, zy)
    far, potential = lax.optimization_barrier((far, potential))

    site, neutral, fh, fl, own, g_mid, g_first, g_second = call(
        functools.partial(backward_kernel, atoms_all),
        [
            ((1, atoms), F32),
            ((32, atoms), F32),
            ((SLAB, 256), BF16),
            ((SLAB, 256), BF16),
            ((3, atoms), F32),
            ((3, 3, 256), F32),
            ((3, 3, 256), F32),
            ((3, 3, 256), F32),
        ],
        [pltpu.VMEM((4, 64, atoms), F32), pltpu.VMEM((3, 32, atoms), F32)],
        spaces="s" + "v" * 16,
        vmem=16,
        flops=5 * 10**9,
        nbytes=4 * 10**6,
    )(
        where,
        far,
        table,
        fx,
        zy,
        potential,
        overlap,
        charge,
        hbar,
        slope,
        vsum,
        geo,
        nbr,
        scalar_weight,
        vector_weight,
        weight,
        pair_t,
    )

    second, first = swapped(g_second, "gy", True), swapped(g_first, "gy", False)
    (base,) = call(
        functools.partial(ewald_kernel, extents),
        [((3, atoms), F32)],
        [pltpu.VMEM((128 * LZ, atoms), BF16)] * 2 + [pltpu.VMEM((rows, atoms), F32) for rows in (8, 8, 64, 64)],
        spaces="s" + "v" * 9,
        vmem=16,
        flops=5 * 10**9,
        nbytes=4 * 10**6,
    )(where, positions, nh, nl, fh, fl, fx, zy, neutral, own)
    first, second, base = lax.optimization_barrier((first, second, base))
    column = g_mid + first + second
    second = swapped(jnp.where(even[0], column[0], column[2]), "gx", True)
    first = swapped(jnp.where(even[0], column[2], column[0]), "gx", False)
    (forces,) = call(
        finish_kernel,
        [((3, atoms), F32)],
        [pltpu.VMEM((3, 3, 256), F32), pltpu.SemaphoreType.DMA((3,))],
        spaces="vaaav",
        vmem=4,
    )(base, column[1], first, second, ghosts)
    return forces, site[0]


def solution(mesh):
    return jax.shard_map(
        shards,
        mesh=mesh,
        in_specs=(
            P(None, ("gx", "gy")),
            P(("gx", "gy")),
            P(("gx", "gy"), None),
            P(("gx", "gy")),
            P(),
            P(),
            P(),
            P(),
            P(),
            P(),
            P(),
            P(),
            P(),
        ),
        out_specs=(P(None, ("gx", "gy")), P(("gx", "gy"))),
        check_vma=False,
    )
```

```python
import functools

import jax
import jax.numpy as jnp
from jax import lax
from jax.experimental import pallas as pl
from jax.experimental.pallas import tpu as pltpu
from jax.sharding import PartitionSpec as P

NB = 8
NS = 8
HIGHEST = lax.Precision.HIGHEST
TWO_PI = 6.283185307179586
BOX_HEIGHT = 4.0
SPLITTING = 2.5
SOFTENING = 0.01
CENTRE_STEP = 0.3
AXES = ("gx", "gy")

HX = 9
LZ = 4
NY = 32
XF = 2 * HX - 1
XROWS = 24
SLAB = XF * 32
UNIT_ROW = 2 * SLAB
TOTAL_ROW = UNIT_ROW + 2 * XROWS
HALF = TOTAL_ROW + 16

F32 = jnp.float32
BF16 = jnp.bfloat16
NT = (((1,), (1,)), ((), ()))
NN = (((1,), (0,)), ((), ()))


def mm(a, b, dims=NN, precision=None):
    return lax.dot_general(a, b, dims, precision=precision, preferred_element_type=F32)


def parts(x):
    high = x.astype(BF16)
    return high, (x - high.astype(F32)).astype(BF16)


def mm3(a, b, dims=NN):
    a_high, a_low = parts(a)
    b_high, b_low = parts(b)
    return mm(a_high, b_high, dims) + (mm(a_low, b_high, dims) + mm(a_high, b_low, dims))


def cos_turns(t):
    r = t - jnp.floor(t + 0.5)
    s = (0.25 - jnp.abs(r)) * TWO_PI
    q = s * s
    p = -2.5052108e-08 + q * 1.6059044e-10
    p = 2.7557319e-06 + q * p
    p = -1.9841270e-04 + q * p
    p = 8.3333333e-03 + q * p
    p = -1.6666667e-01 + q * p
    return s + s * (q * p)


def silu_parts(x):
    gate = 1.0 / (1.0 + jnp.exp(-x))
    return x * gate, gate * (1.0 + x * (1.0 - gate))


def iota(shape, dim):
    return lax.broadcasted_iota(jnp.int32, shape, dim)


def call(kernel, outs, scratch=(), spaces="", flops=0, nbytes=0, vmem=56):
    known = {"s": pltpu.SMEM, "v": pltpu.VMEM, "a": pl.ANY, "h": pltpu.HBM}
    return pl.pallas_call(
        kernel,
        in_specs=[pl.BlockSpec(memory_space=known[letter]) for letter in spaces],
        out_shape=[jax.ShapeDtypeStruct(s, d) for s, d in outs],
        scratch_shapes=list(scratch),
        compiler_params=pltpu.CompilerParams(vmem_limit_bytes=vmem * 2**20),
        cost_estimate=pl.CostEstimate(flops=flops, bytes_accessed=nbytes, transcendentals=0),
    )


def border_kernel(pos_ref, species_ref, ghost_ref, out_ref, tab_ref):
    atoms = pos_ref.shape[1]
    tab_ref[0:3, :] = pos_ref[...]
    tab_ref[3:4, :] = species_ref[...].astype(F32)
    for part in range(ghost_ref.shape[1] // 128):
        lanes = pl.ds(128 * part, 128)
        index = jnp.broadcast_to(ghost_ref[:, lanes], (8, 128))
        high, low = index >> 7, index & 127
        value = jnp.zeros((8, 128), F32)
        for block in range(atoms // 128):
            source = tab_ref[:, pl.ds(128 * block, 128)]
            value = jnp.where(high == block, jnp.take_along_axis(source, low, axis=1), value)
        out_ref[:, lanes] = value[0:4]


def waves(grid, where_ref, pos_ref):
    extent_x, extent_y = grid
    atoms = pos_ref.shape[1]
    u, v = where_ref[0], where_ref[1]
    x, y, z = pos_ref[0:1, :], pos_ref[1:2, :], pos_ref[2:3, :]

    row = iota((XROWS, atoms), 0)
    order = jnp.where(row < HX, row, row - (HX - 1))
    whole = lax.rem(order * u, extent_x).astype(F32)
    order = order.astype(F32)
    turn_x = (order * x + whole) / extent_x - jnp.where(row < HX, 0.0, 0.25)
    rate_x = jnp.where(row < XF, order * (TWO_PI / extent_x), 0.0)

    row = iota((2 * LZ, atoms), 0)
    whole = lax.rem(v, 2 * extent_y).astype(F32)
    turn_z = ((row >> 1) + 1).astype(F32) * z * (1.0 / BOX_HEIGHT) - (y + whole) * (0.5 / extent_y)
    turn_z = turn_z - 0.25 * (row & 1).astype(F32)

    row = iota((2 * NY, atoms), 0)
    twice = 2 * (row & (NY - 1)) + 1
    whole = lax.rem(twice * v, 2 * extent_y).astype(F32)
    twice = twice.astype(F32)
    turn_y = (twice * y + whole) * (0.5 / extent_y) - jnp.where(row < NY, 0.0, 0.25)
    return turn_x, rate_x, turn_z, turn_y, twice * (0.5 * TWO_PI / extent_y)


def prepare_kernel(
    grid,
    where_ref,
    pos_ref,
    embed_ref,
    radial_ref,
    message_ref,
    readout_ref,
    x_out,
    zy_out,
    unit_out,
    weight_out,
    weight_t_out,
    embed_out,
    readout_out,
):
    turn_x, _, turn_z, turn_y, _ = waves(grid, where_ref, pos_ref)
    fx = jnp.where(iota(turn_x.shape, 0) < XF, cos_turns(turn_x), 0.0)
    fz, fy = cos_turns(turn_z), cos_turns(turn_y)
    x_out[...] = fx

    for l in range(LZ):
        zy = jnp.concatenate([fz[2 * l : 2 * l + 1] * fy, fz[2 * l + 1 : 2 * l + 2] * fy], axis=0)
        high, low = parts(zy)
        zy_out[0, 128 * l : 128 * l + 128] = high
        zy_out[1, 128 * l : 128 * l + 128] = low
        unit_out[l] = mm(fx, zy, NT, HIGHEST)

    embed = embed_ref[...].T
    message = mm(message_ref[...].T, embed, NN, HIGHEST)
    embed_out[...] = embed
    readout_out[...] = jnp.broadcast_to(readout_ref[...], (8, 128)).T
    col = iota((NB, 64), 1)
    sub = iota((NB, 64), 0)
    pick_b = ((col >> 3) == sub).astype(F32)
    pick_s = ((col & 7) == sub).astype(F32)
    spread = mm(message, pick_s, NN, HIGHEST)
    radial = radial_ref[...].T
    channels = message.shape[0]
    for which in range(2):
        weight = mm(radial[which * channels : (which + 1) * channels], pick_b, NN, HIGHEST) * spread
        weight_out[which] = weight
        weight_t_out[which] = weight.T


def later_kernel(
    grid,
    atoms_all,
    wave_ref,
    charge_ref,
    table_out,
    charge_out,
):
    extent_x, extent_y = grid

    step = wave_ref.shape[1]
    order = iota((40, step), 0)
    along_x, along_y, along_z = wave_ref[0:1, :], wave_ref[1:2, :], wave_ref[2:3, :]
    matches_z = ((order & 3) + 1 == along_z) & (order < HX * LZ)
    plus = matches_z & ((order >> 2) == along_x)
    minus = matches_z & ((order >> 2) == -along_x) & (order >= LZ)
    lanes = iota((NY, step), 0)
    up = (lanes == along_y).astype(F32).astype(BF16)
    down = (-lanes - 1 == along_y).astype(F32).astype(BF16)
    both = jnp.concatenate([up] * 4 + [down] * 4, axis=0)
    plus = mm(plus.astype(F32).astype(BF16), both, NT)
    minus = mm(minus.astype(F32).astype(BF16), both, NT)
    order = iota((40, 128), 0)
    lanes = iota((40, 128), 1)
    wave_b = (lanes & (NY - 1)).astype(F32)
    kx = (order >> 2).astype(F32) * (TWO_PI / extent_x)
    kz = ((order & 3) + 1).astype(F32) * (TWO_PI / BOX_HEIGHT)

    def weights(ky):
        squared = kx * kx + ky * ky + kz * kz
        return jnp.exp(-squared / (4.0 * SPLITTING**2)) / squared / atoms_all

    green_up = weights(wave_b * (TWO_PI / extent_y))
    green_down = weights((wave_b + 1.0) * (TWO_PI / extent_y))
    pp, pm = green_up * plus[:, 0:128], green_down * plus[:, 128:256]
    mp, mn = green_up * minus[:, 0:128], green_down * minus[:, 128:256]
    quarter = lanes >> 5
    sign_t = jnp.where((quarter == 1) | (quarter == 2), 1.0, -1.0)
    sign_st = jnp.where((quarter & 1) == 1, 1.0, -1.0)
    sign_s = jnp.where(quarter >= 2, 1.0, -1.0)
    table_out[0] = (pp + pm) + (mp + mn)
    table_out[1] = sign_t * ((pp - pm) + (mp - mn))
    table_out[2] = sign_st * ((pp - pm) - (mp - mn))
    table_out[3] = sign_s * ((pp + pm) - (mp + mn))

    charge_out[...] = charge_ref[...].T


def basis_terms(dist, rho, live):
    envelope = jnp.exp(-0.25 * rho) * live
    out = []
    for b in range(NB):
        off = dist - CENTRE_STEP * b
        out.append((jnp.exp(off * off * (-0.5 / CENTRE_STEP**2)) * envelope, off))
    return out


def forward_kernel(
    where_ref,
    pos_ref,
    species_ref,
    mid_ref,
    first_ref,
    second_ref,
    nbr_ref,
    embed_ref,
    pair_ref,
    scalar_ref,
    vector_ref,
    hidden_ref,
    readout_ref,
    weight_ref,
    x_ref,
    zy_ref,
    unit_ref,
    charge_out,
    hbar_out,
    slope_out,
    vsum_out,
    geo_out,
    send_out,
    tab_ref,
    moment_ref,
    qh_ref,
    ql_ref,
):
    atoms = pos_ref.shape[1]
    tiles = atoms // 128
    for c in range(3):
        for j in range(tiles):
            tab_ref[c, j : j + 1, :] = pos_ref[c : c + 1, pl.ds(128 * j, 128)]
    for j in range(tiles):
        tab_ref[3, j : j + 1, :] = species_ref[:, pl.ds(128 * j, 128)].astype(F32)
    even = (where_ref[0] & 1) == 0
    for j in range(3):
        first, second = first_ref[j], second_ref[j]
        prev, after = jnp.where(even, second, first), jnp.where(even, first, second)
        for i, block in enumerate((prev, mid_ref[j], after)):
            shifts = (i - 1.0, j - 1.0, 0.0, 0.0)
            for c in range(4):
                for h in range(2):
                    at = tiles + 2 * (3 * i + j) + h
                    tab_ref[c, at : at + 1, :] = block[c : c + 1, 128 * h : 128 * h + 128] + shifts[c]

    def lane_tile(t, carry):
        lanes = pl.ds(pl.multiple_of(t * 128, 128), 128)
        for tile in range(4):
            index = nbr_ref[pl.ds(8 * tile, 8), lanes]
            live = (index >= 0).astype(F32)
            index = jnp.maximum(index, 0)
            high, low = index >> 7, index & 127
            value = [jnp.zeros((8, 128), F32) for _ in range(4)]
            for block in range(tiles + 18):
                if block // 2 == tiles // 2 + 4:
                    continue
                here = high == block
                for c in range(4):
                    source = jnp.broadcast_to(tab_ref[c, block : block + 1, :], (8, 128))
                    value[c] = jnp.where(here, jnp.take_along_axis(source, low, axis=1), value[c])
            rx, ry, rz = (value[c] - pos_ref[c : c + 1, lanes] for c in range(3))
            rho = rx * rx + ry * ry + rz * rz
            dist = jnp.sqrt(rho + SOFTENING)
            inv = 1.0 / dist
            rows = pl.ds(8 * tile, 8)
            geo_out[0, rows, lanes] = rx * inv
            geo_out[1, rows, lanes] = ry * inv
            geo_out[2, rows, lanes] = rz * inv
            geo_out[3, rows, lanes] = dist
            geo_out[4, rows, lanes] = rho
            geo_out[5, rows, lanes] = value[3]
            geo_out[6, rows, lanes] = live
        dist = geo_out[3, :, lanes]
        terms = basis_terms(dist, geo_out[4, :, lanes], geo_out[6, :, lanes])
        kind = geo_out[5, :, lanes]
        for f in range(4):
            for b in range(NB):
                value = terms[b][0] if f == 0 else terms[b][0] * geo_out[f - 1, :, lanes]
                rows = []
                for s in range(NS):
                    chosen = jnp.where(kind == float(s), value, 0.0)
                    rows.append((chosen[0:8] + chosen[8:16]) + (chosen[16:24] + chosen[24:32]))
                for step in (4, 2, 1):
                    here = (iota((8, 128), 0) & step) == 0
                    rows = [
                        jnp.where(here, one + pltpu.roll(one, 8 - step, 0), two + pltpu.roll(two, step, 0))
                        for one, two in zip(rows[: len(rows) // 2], rows[len(rows) // 2 :])
                    ]
                moment_ref[f, 8 * b : 8 * b + 8, lanes] = rows[0]
        return carry

    lax.fori_loop(0, tiles, lane_tile, 0, unroll=2)

    def gathered(f):
        return mm3(pair_ref[0 if f == 0 else 1], moment_ref[f])

    scalar_sum = gathered(0)
    norm = None
    for c in range(3):
        vector = gathered(c + 1)
        vsum_out[c] = vector
        norm = vector * vector if norm is None else norm + vector * vector
    update = mm3(scalar_ref[...].T, scalar_sum) + mm3(vector_ref[...].T, norm)
    feature = jnp.zeros_like(update)
    kinds = species_ref[...]
    for s in range(NS):
        feature = jnp.where(kinds == s, embed_ref[:, s : s + 1], feature)
    act, slope = silu_parts(update)
    slope_out[...] = slope
    hidden = feature + act
    act, slope = silu_parts(mm3(hidden_ref[...].T, hidden))
    readout = readout_ref[:, 0:1]
    charge_out[32:33, :] = jnp.sum(act * readout, axis=0, keepdims=True)
    hbar_out[...] = mm3(hidden_ref[...], slope * readout)
    charges = mm3(weight_ref[...], hidden)
    charge_out[0:32, :] = charges
    charge_out[33:40, :] = jnp.zeros((7, atoms), F32)

    half_sums(1 - (where_ref[0] & 1), charges, x_ref, zy_ref, unit_ref, send_out, qh_ref, ql_ref)


def half_sums(half, charges, x_ref, zy_ref, unit_ref, out, qh_ref, ql_ref):
    total = jnp.sum(charges, axis=1, keepdims=True)
    local = total * (1.0 / charges.shape[1])
    centred = charges - local
    for k in range(XF):
        high, low = parts(centred * x_ref[k : k + 1, :])
        qh_ref[32 * k : 32 * k + 32, :] = high
        ql_ref[32 * k : 32 * k + 32, :] = low
    high, low = qh_ref[...], ql_ref[...]
    near, rest = (zy_ref[part, pl.ds(pl.multiple_of(256 * half, 256), 256), :] for part in range(2))
    slabs = mm(high, near, NT) + (mm(low, near, NT) + mm(high, rest, NT))
    for n in range(2):
        unit = unit_ref[2 * half + n]
        for k in range(XF):
            at = SLAB * n + 32 * k
            value = slabs[32 * k : 32 * k + 32, 128 * n : 128 * n + 128]
            out[at : at + 32, :] = value + local * unit[k : k + 1]
        out[UNIT_ROW + XROWS * n : UNIT_ROW + XROWS * (n + 1), :] = unit
    out[TOTAL_ROW:HALF, :] = jnp.where(iota((16, 128), 1) < 64, total[0:16], total[16:32])


def keep_kernel(where_ref, charge_ref, x_ref, zy_ref, unit_ref, keep_out, qh_ref, ql_ref):
    half_sums(where_ref[0] & 1, charge_ref[0:32, :], x_ref, zy_ref, unit_ref, keep_out, qh_ref, ql_ref)


def quarters(x, which):
    lane = iota(x.shape, 1)
    if which == 2:
        return pltpu.roll(x, 64, 1)
    even = ((lane >> 5) & 1) == 0
    if which == 1:
        return jnp.where(even, pltpu.roll(x, 96, 1), pltpu.roll(x, 32, 1))
    return jnp.where(even, pltpu.roll(x, 32, 1), pltpu.roll(x, 96, 1))


def contribution(half, ref, table_ref, x_ref, zy_ref, vh_out, vl_out, atoms_all):
    ends = ref[TOTAL_ROW:HALF, :]
    mean = jnp.concatenate([ends[:, 0:1], ends[:, 64:65]], axis=0) * (1.0 / atoms_all)

    def put(n, k, value):
        rows = pl.ds(pl.multiple_of(k * 32, 32), 32)
        high, low = parts(value)
        vh_out[rows, 128 * n : 128 * n + 128] = high
        vl_out[rows, 128 * n : 128 * n + 128] = low

    def tile_of(n, k):
        unit = ref[pl.ds(UNIT_ROW + XROWS * n + k, 1), :]
        rows = pl.ds(pl.multiple_of(SLAB * n + k * 32, 32), 32)
        return ref[rows, :] - mean * unit, unit

    overlap = jnp.zeros((32, 128), F32)
    for n in range(2):
        cos_tile, unit = tile_of(n, 0)
        g0, gt = (table_ref[t, pl.ds(2 * half + n, 1), :] for t in range(2))
        value = g0 * cos_tile + gt * quarters(cos_tile, 3)
        overlap = overlap + value * unit
        put(n, 0, value)

    def mix(a, overlap):
        for n in range(2):
            cos_tile, cos_unit = tile_of(n, a)
            sin_tile, sin_unit = tile_of(n, a + HX - 1)
            g0, gt, gst, gs = (table_ref[t, pl.ds(a * LZ + 2 * half + n, 1), :] for t in range(4))
            value = (g0 * cos_tile + gt * quarters(cos_tile, 3)) + (
                gst * quarters(sin_tile, 1) + gs * quarters(sin_tile, 2)
            )
            overlap = overlap + value * cos_unit
            put(n, a, value)
            value = (g0 * sin_tile + gt * quarters(sin_tile, 3)) - (
                gst * quarters(cos_tile, 1) + gs * quarters(cos_tile, 2)
            )
            overlap = overlap + value * sin_unit
            put(n, a + HX - 1, value)
        return overlap

    overlap = lax.fori_loop(1, HX, mix, overlap, unroll=8)
    at = pl.ds(pl.multiple_of(256 * half, 256), 256)
    high, low = zy_ref[0, at, :], zy_ref[1, at, :]
    spread = mm(vh_out[...], high) + (mm(vl_out[...], high) + mm(vh_out[...], low))
    potential = jnp.zeros((32, zy_ref.shape[2]), F32)
    for k in range(XF):
        potential = potential + x_ref[k : k + 1, :] * spread[32 * k : 32 * k + 32]
    return mean, potential, overlap


def near_kernel(
    atoms_all, where_ref, near_ref, table_ref, x_ref, zy_ref, vh_out, vl_out, potential_out, overlap_out
):
    half = where_ref[0] & 1
    _, potential, overlap = contribution(half, near_ref, table_ref, x_ref, zy_ref, vh_out, vl_out, atoms_all)
    potential_out[...] = potential
    overlap_out[...] = overlap


def backward_kernel(
    atoms_all,
    where_ref,
    far_ref,
    table_ref,
    x_ref,
    zy_ref,
    potential_ref,
    overlap_ref,
    charge_ref,
    hbar_ref,
    slope_ref,
    vsum_ref,
    geo_ref,
    nbr_ref,
    scalar_ref,
    vector_ref,
    weight_ref,
    pair_ref,
    site_out,
    neutral_out,
    vh_out,
    vl_out,
    own_out,
    mid_out,
    first_out,
    second_out,
    g_ref,
    rbar_ref,
):
    atoms = nbr_ref.shape[1]
    tiles = atoms // 128
    half = 1 - (where_ref[0] & 1)
    mean, potential, overlap = contribution(half, far_ref, table_ref, x_ref, zy_ref, vh_out, vl_out, atoms_all)
    potential = potential + potential_ref[...]
    overlap = overlap + overlap_ref[...]
    potential_mean = jnp.sum(overlap, axis=1, keepdims=True) * (1.0 / atoms_all)
    neutral = charge_ref[0:32, :] - mean
    neutral_out[...] = neutral
    site_out[...] = charge_ref[32:33, :] + jnp.sum(neutral * potential, axis=0, keepdims=True)
    charge_bar = 2.0 * (potential - potential_mean)
    update_bar = (hbar_ref[...] + mm3(weight_ref[...], charge_bar)) * slope_ref[...]
    scalar_bar = mm3(scalar_ref[...], update_bar)
    norm_bar = 2.0 * mm3(vector_ref[...], update_bar)
    g_ref[0] = mm3(pair_ref[0], scalar_bar)
    for c in range(3):
        g_ref[c + 1] = mm3(pair_ref[1], vsum_ref[c] * norm_bar)

    def slots(t, carry):
        lanes = pl.ds(pl.multiple_of(t * 128, 128), 128)
        own = [jnp.zeros((8, 128), F32) for _ in range(3)]
        for tile in range(4):
            rows = pl.ds(8 * tile, 8)
            unit = [geo_ref[c, rows, lanes] for c in range(3)]
            dist = geo_ref[3, rows, lanes]
            kind = geo_ref[5, rows, lanes].astype(jnp.int32)
            terms = basis_terms(dist, geo_ref[4, rows, lanes], geo_ref[6, rows, lanes])
            inv = 1.0 / dist
            ubar = [jnp.zeros((8, 128), F32) for _ in range(3)]
            plain = jnp.zeros((8, 128), F32)
            tilted = jnp.zeros((8, 128), F32)
            for b in range(NB):
                value, off = terms[b]
                picked = [
                    jnp.take_along_axis(g_ref[f, 8 * b : 8 * b + 8, lanes], kind, axis=0) for f in range(4)
                ]
                bar = picked[0]
                for c in range(3):
                    bar = bar + unit[c] * picked[c + 1]
                    ubar[c] = ubar[c] + value * picked[c + 1]
                bar = bar * value
                plain = plain + bar
                tilted = tilted + bar * off
            along = ubar[0] * unit[0] + ubar[1] * unit[1] + ubar[2] * unit[2]
            dist_bar = tilted * (-1.0 / CENTRE_STEP**2) - along * inv
            radial = dist * (2.0 * (-0.25 * plain) + dist_bar * inv)
            for c in range(3):
                bar = ubar[c] * inv + unit[c] * radial
                rbar_ref[c, rows, lanes] = bar
                own[c] = own[c] + bar
        for c in range(3):
            own_out[c : c + 1, lanes] = -jnp.sum(own[c], axis=0, keepdims=True)
        return carry

    lax.fori_loop(0, tiles, slots, 0)

    block_rows = 24
    rows_high = iota((block_rows, atoms), 0)
    rows_low = iota((128, atoms), 0)

    def scatter(s, total):
        index = jnp.maximum(nbr_ref[pl.ds(s, 1), :], 0)
        at_high = rows_high == (index >> 7)
        at_low = jnp.where(rows_low == (index & 127), 1.0, 0.0).astype(BF16)
        pieces = []
        for c in range(3):
            value = rbar_ref[c, pl.ds(s, 1), :]
            high = value.astype(BF16).astype(F32)
            pieces.append(jnp.where(at_high, high, 0.0))
            pieces.append(jnp.where(at_high, value - high, 0.0))
        left = jnp.concatenate(pieces, axis=0).astype(BF16)
        return total + mm(left, at_low, NT)

    even = (where_ref[1] & 1) == 0
    total = lax.fori_loop(0, nbr_ref.shape[0], scatter, jnp.zeros((6 * block_rows, 128), F32), unroll=16)
    for c in range(3):
        at = 2 * block_rows * c
        table = total[at : at + block_rows] + total[at + block_rows : at + 2 * block_rows]
        for j in range(tiles):
            lanes = pl.ds(128 * j, 128)
            own_out[c : c + 1, lanes] = own_out[c : c + 1, lanes] + table[j : j + 1]
        for i in range(3):
            for h in range(2):
                lanes = slice(128 * h, 128 * h + 128)
                prev, mid, after = (table[row : row + 1] for row in (tiles + 2 * (3 * i + j) + h for j in range(3)))
                mid_out[i, c : c + 1, lanes] = mid
                first_out[i, c : c + 1, lanes] = jnp.where(even, after, prev)
                second_out[i, c : c + 1, lanes] = jnp.where(even, prev, after)


def ewald_kernel(
    grid,
    where_ref,
    pos_ref,
    nh_ref,
    nl_ref,
    fh_ref,
    fl_ref,
    x_ref,
    zy_ref,
    neutral_ref,
    own_ref,
    out_ref,
    high_ref,
    low_ref,
    z_ref,
    dz_ref,
    y_ref,
    dy_ref,
):
    extent_x, extent_y = grid
    core = where_ref[0] & 1
    neutral = neutral_ref[...]
    turn_x, rate_x, turn_z, turn_y, rate_y = waves(grid, where_ref, pos_ref)
    first = core == 0
    coefficients = [
        (jnp.where(first, nh_ref[...], fh_ref[...]), jnp.where(first, nl_ref[...], fl_ref[...]), slice(0, 256)),
        (jnp.where(first, fh_ref[...], nh_ref[...]), jnp.where(first, fl_ref[...], nl_ref[...]), slice(256, 512)),
    ]

    def total(c, functions, high_ref, low_ref):
        spread = None
        for high, low, at in coefficients:
            near, rest = high_ref[at, :], low_ref[at, :]
            term = mm(high, near) + (mm(low, near) + mm(high, rest))
            spread = term if spread is None else spread + term
        field = None
        for k in range(XF):
            term = functions[k : k + 1, :] * spread[32 * k : 32 * k + 32]
            field = term if field is None else field + term
        out_ref[c : c + 1, :] = own_ref[c : c + 1, :] + 2.0 * jnp.sum(neutral * field, axis=0, keepdims=True)

    total(0, cos_turns(turn_x + 0.25) * rate_x, zy_ref.at[0], zy_ref.at[1])
    z_ref[...] = cos_turns(turn_z)
    dz_ref[...] = cos_turns(turn_z + 0.25)
    y_ref[...] = cos_turns(turn_y)
    dy_ref[...] = cos_turns(turn_y + 0.25) * rate_y
    for c in (2, 1):
        for at in range(2 * LZ):
            turned = dz_ref[at : at + 1, :]
            if c == 2:
                value = (TWO_PI / BOX_HEIGHT * (at // 2 + 1)) * turned * y_ref[...]
            else:
                value = z_ref[at : at + 1, :] * dy_ref[...] - (0.5 * TWO_PI / extent_y) * turned * y_ref[...]
            high, low = parts(value)
            high_ref[64 * at : 64 * at + 64, :] = high
            low_ref[64 * at : 64 * at + 64, :] = low
        total(c, x_ref, high_ref, low_ref)


def finish_kernel(base_ref, mid_ref, first_ref, second_ref, ghost_ref, out_ref):
    atoms = base_ref.shape[1]
    returned = mid_ref[...] + first_ref[...] + second_ref[...]
    high = returned.astype(BF16).astype(F32)
    rest = returned - high
    middle = rest.astype(BF16).astype(F32)
    split = jnp.concatenate([high, middle, rest - middle, jnp.zeros((7, 256), F32)], axis=0).astype(BF16)
    at = jnp.where(iota((atoms, 256), 0) == ghost_ref[...], 1.0, 0.0).astype(BF16)
    spread = mm(split, at, NT)
    out_ref[...] = -(base_ref[...] + ((spread[0:3] + spread[3:6]) + spread[6:9]))


def swapped(array, axis, far):
    n = lax.axis_size(axis)
    pairs = [(i, (i + (1 if i % 2 else -1)) % n if far else i ^ 1) for i in range(n)]
    return lax.ppermute(array, axis, pairs)


def along_z(array, flip):
    first, second = lax.axis_size("gx"), lax.axis_size("gy")
    pairs = []
    for device in range(first * second):
        u, v = divmod(device, second)
        z = (v // 16 * 4 + u // 2) ^ flip
        pairs.append((device, (z % 4 * 2 + u % 2) * second + z // 4 * 16 + v % 16))
    return lax.ppermute(array, AXES, pairs)


def across_plane(array):
    planes = [list(range(16 * k, 16 * k + 16)) for k in range(lax.axis_size("gy") // 16)]
    return lax.all_to_all(array, "gy", 0, 0, tiled=True, axis_index_groups=planes)


def reduced(keep, got):
    got = across_plane((keep + got).reshape(16, -1, 128))
    return sum((got[k] for k in range(1, 16)), got[0])


def shards(
    positions,
    species,
    neighbours,
    ghost_index,
    wave_index,
    embedding,
    radial_weight,
    message_weight,
    scalar_weight,
    vector_weight,
    readout_hidden,
    readout_vector,
    charge_weight,
):
    atoms = positions.shape[1]
    extents = lax.axis_size("gx"), lax.axis_size("gy")
    atoms_all = atoms * extents[0] * extents[1]
    where = jnp.stack([lax.axis_index("gx"), lax.axis_index("gy")])
    kinds = species[None]
    ghosts = ghost_index[None]

    (border,) = call(border_kernel, [((4, 256), F32)], [pltpu.VMEM((8, atoms), F32)], spaces="vvv", vmem=4)(positions, kinds, ghosts)
    even = [(where[axis] & 1) == 0 for axis in range(2)]
    second, first = swapped(border, "gy", True), swapped(border, "gy", False)
    fx, zy, unit, pair, pair_t, embed, readout = call(
        functools.partial(prepare_kernel, extents),
        [
            ((XROWS, atoms), F32),
            ((2, 128 * LZ, atoms), BF16),
            ((LZ, XROWS, 128), F32),
            ((2, 128, 64), F32),
            ((2, 64, 128), F32),
            ((128, 8), F32),
            ((128, 8), F32),
        ],
        spaces="svvvvv",
        vmem=16,
        flops=10**9,
        nbytes=2 * 10**6,
    )(where, positions, embedding, radial_weight, message_weight, readout_vector[None])
    second, first, zy = lax.optimization_barrier((second, first, zy))
    mid = jnp.stack([jnp.where(even[1], second, first), border, jnp.where(even[1], first, second)])
    second, first = swapped(mid, "gx", True), swapped(mid, "gx", False)

    nbr = neighbours.T
    charge_t = charge_weight.T
    charge, hbar, slope, vsum, geo, send = call(
        forward_kernel,
        [
            ((40, atoms), F32),
            ((128, atoms), F32),
            ((128, atoms), F32),
            ((3, 128, atoms), F32),
            ((7, 32, atoms), F32),
            ((HALF, 128), F32),
        ],
        [
            pltpu.VMEM((4, 24, 128), F32),
            pltpu.VMEM((4, 64, atoms), F32),
            pltpu.VMEM((SLAB, atoms), BF16),
            pltpu.VMEM((SLAB, atoms), BF16),
        ],
        spaces="s" + "v" * 16,
        vmem=16,
        flops=5 * 10**9,
        nbytes=4 * 10**6,
    )(
        where,
        positions,
        kinds,
        mid,
        first,
        second,
        nbr,
        embed,
        pair,
        scalar_weight,
        vector_weight,
        readout_hidden,
        readout,
        charge_t,
        fx,
        zy,
        unit,
    )

    got = swapped(send, "gx", False)
    (keep,) = call(
        keep_kernel,
        [((HALF, 128), F32)],
        [pltpu.VMEM((SLAB, atoms), BF16), pltpu.VMEM((SLAB, atoms), BF16)],
        spaces="svvvv",
        vmem=16,
        flops=10**9,
        nbytes=2 * 10**6,
    )(where, charge, fx, zy, unit)
    got, keep = lax.optimization_barrier((got, keep))
    keep = reduced(keep, got)
    keep = keep + along_z(keep, 1)
    got = along_z(keep, 2)
    keep, waves_late, charge_late = lax.optimization_barrier((keep, wave_index, charge_t))
    table, weight = call(
        functools.partial(later_kernel, extents, atoms_all),
        [((4, 40, 128), F32), ((128, 32), F32)],
        spaces="vv",
        vmem=16,
        flops=10**9,
        nbytes=2 * 10**6,
    )(waves_late, charge_late)
    got, table, weight = lax.optimization_barrier((got, table, weight))
    keep = keep + got
    keep = keep + along_z(keep, 6)
    near = across_plane(jnp.broadcast_to(keep, (16,) + keep.shape)).reshape(-1, 128)
    far = swapped(near, "gx", False)
    nh, nl, potential, overlap = call(
        functools.partial(near_kernel, atoms_all),
        [((SLAB, 256), BF16), ((SLAB, 256), BF16), ((32, atoms), F32), ((32, 128), F32)],
        spaces="svvvv",
        vmem=16,
        flops=10**9,
        nbytes=2 * 10**6,
    )(where, near, table, fx, zy)
    far, potential = lax.optimization_barrier((far, potential))

    site, neutral, fh, fl, own, g_mid, g_first, g_second = call(
        functools.partial(backward_kernel, atoms_all),
        [
            ((1, atoms), F32),
            ((32, atoms), F32),
            ((SLAB, 256), BF16),
            ((SLAB, 256), BF16),
            ((3, atoms), F32),
            ((3, 3, 256), F32),
            ((3, 3, 256), F32),
            ((3, 3, 256), F32),
        ],
        [pltpu.VMEM((4, 64, atoms), F32), pltpu.VMEM((3, 32, atoms), F32)],
        spaces="s" + "v" * 16,
        vmem=16,
        flops=5 * 10**9,
        nbytes=4 * 10**6,
    )(
        where,
        far,
        table,
        fx,
        zy,
        potential,
        overlap,
        charge,
        hbar,
        slope,
        vsum,
        geo,
        nbr,
        scalar_weight,
        vector_weight,
        weight,
        pair_t,
    )

    second, first = swapped(g_second, "gy", True), swapped(g_first, "gy", False)
    (base,) = call(
        functools.partial(ewald_kernel, extents),
        [((3, atoms), F32)],
        [pltpu.VMEM((128 * LZ, atoms), BF16)] * 2 + [pltpu.VMEM((rows, atoms), F32) for rows in (8, 8, 64, 64)],
        spaces="s" + "v" * 9,
        vmem=16,
        flops=5 * 10**9,
        nbytes=4 * 10**6,
    )(where, positions, nh, nl, fh, fl, fx, zy, neutral, own)
    first, second, base = lax.optimization_barrier((first, second, base))
    column = g_mid + first + second
    second = swapped(jnp.where(even[0], column[0], column[2]), "gx", True)
    first = swapped(jnp.where(even[0], column[2], column[0]), "gx", False)
    (forces,) = call(
        finish_kernel,
        [((3, atoms), F32)],
        spaces="vvvvv",
        vmem=4,
    )(base, column[1], first, second, ghosts)
    return forces, site[0]


def solution(mesh):
    return jax.shard_map(
        shards,
        mesh=mesh,
        in_specs=(
            P(None, ("gx", "gy")),
            P(("gx", "gy")),
            P(("gx", "gy"), None),
            P(("gx", "gy")),
            P(),
            P(),
            P(),
            P(),
            P(),
            P(),
            P(),
            P(),
            P(),
        ),
        out_specs=(P(None, ("gx", "gy")), P(("gx", "gy"))),
        check_vma=False,
    )
```
